256 devices in a mesh: row: 16 (over y, z_hi), col: 16 (over z_lo, x, core).
Axes of the slice: x: 4, y: 4, z: 8 (z_hi: 4, z_lo: 2; z = z_hi * 2 + z_lo), core: 2. Of those that a mesh axis runs over, the one named last changes fastest.
Arguments:
- pair: bfloat16 [512, 512, 128], P('row', 'col'), may hold values from -400 to 400, as said below
- cotangent: bfloat16 [512, 512, 128], P('row', 'col'), may hold values from -6 to 6
- in_weight: bfloat16 [128, 512], replicated, may hold values from -0.5 to 0.5
- gate_weight: bfloat16 [128, 128], replicated, may hold values from -0.5 to 0.5
- out_weight: bfloat16 [128, 128], replicated, may hold values from -0.5 to 0.5
Outputs:
- pair_grad: bfloat16 [512, 512, 128], P('row', 'col')
- in_grad: float32 [128, 512], replicated
- gate_grad: float32 [128, 128], replicated
- out_grad: float32 [128, 128], replicated
The draws below stay inside these ranges and needn't reach their ends.
Inputs may be any that keep to these rules, and one draw needn't show every extreme that they name: Each entry is a bounded noise value times a positive scale of its pair and a positive scale of its channel.
All inputs are finite; a program needn't handle non-finite values.
Results may differ from the reference program's by a relative error of at most 0.0088.
Values may be sent and summed in bfloat16 or wider, within the bound.
No kernel may reach another device: no remote copies, remote signals or barrier semaphores. Data moves between devices by JAX's collectives and lax.ppermute only.
A program may use at most 128 MiB of HBM per device.

```python
import math
import jax
import jax.numpy as jnp
from jax import lax

C = 128
H = 128
N = 512


def draw_pair(key, part):
    key = jax.random.fold_in(key, 11)
    key_noise, key_pair, key_chan = jax.random.split(key, 3)
    noise = jax.random.truncated_normal(key_noise, -4.0, 4.0, (N, N, C), jnp.float32)
    pair_scale = jnp.exp(jax.random.uniform(key_pair, (N, N, 1), jnp.float32) * math.log(10.0))
    chan_scale = jnp.exp(jax.random.uniform(key_chan, (C,), jnp.float32) * math.log(10.0))
    return (noise * pair_scale * chan_scale).astype(jnp.bfloat16)


def block_scale(rng, extent, shards, smallest, top_value):
    gain = 1.0
    for dim, parts in shards:
        draws = jax.random.uniform(jax.random.fold_in(jax.random.fold_in(rng, 6), dim), (parts,), jnp.float32, smallest / len(shards), top_value / len(shards))
        gain = gain * jnp.repeat(jnp.exp(draws), extent[dim] // parts).reshape((-1,) + (1,) * (len(extent) - 1 - dim))
    return gain


def centred(own_key, dims, scale, most, pieces=(), held_as=jnp.bfloat16):
    entries = scale * jax.random.normal(own_key, dims, jnp.float32)
    if pieces:
        entries = entries * block_scale(own_key, dims, pieces, -0.22, 0.18)
    return jnp.clip(entries, -most, most).astype(held_as)


def setup_inputs(seed: int = 0) -> dict:
    splits = jax.random.split(jax.random.key(seed), 6)
    return {
        "pair": draw_pair(jax.random.fold_in(splits[5], 71), 0),
        "cotangent": centred(splits[1], (N, N, C), 1.0, 6.0, ((0, 16), (1, 16))),
        "in_weight": centred(splits[2], (C, 4 * H), C ** -0.5, 0.5),
        "gate_weight": centred(splits[3], (C, C), C ** -0.5, 0.5),
        "out_weight": centred(splits[4], (H, C), H ** -0.5, 0.5),
    }


def apply_layer_norm(values):
    center = values - lax.optimization_barrier(jnp.mean(values, axis=-1, keepdims=True))
    scale = lax.rsqrt(lax.optimization_barrier(jnp.mean(center * center, axis=-1, keepdims=True)) + 1e-05)
    return (center * scale, scale)

def layer_norm_backward(grad, normal, scale):
    first = lax.optimization_barrier(jnp.mean(grad, axis=-1, keepdims=True))
    second = lax.optimization_barrier(jnp.mean(grad * normal, axis=-1, keepdims=True))
    return scale * (grad - first - normal * second)

def flat_dot(left, right):
    width = left.shape[-1]
    result = jnp.dot(left.reshape(-1, width), right, preferred_element_type=jnp.float32)
    return result.reshape(left.shape[:-1] + (right.shape[-1],))

def reference(pair, cotangent, in_weight, gate_weight, out_weight):
    zhat, zinv = apply_layer_norm(pair.astype(jnp.float32))
    normed = zhat.astype(jnp.bfloat16)
    proj = flat_dot(normed, in_weight)
    a_val = proj[..., 0:H]
    sig_a = jax.nn.sigmoid(proj[..., H:2 * H])
    b_val = proj[..., 2 * H:3 * H]
    sig_b = jax.nn.sigmoid(proj[..., 3 * H:4 * H])
    a_half = (sig_a * a_val).astype(jnp.bfloat16)
    b_half = (sig_b * b_val).astype(jnp.bfloat16)
    a_full = a_half.astype(jnp.float32)
    b_full = b_half.astype(jnp.float32)
    hidden_state = jnp.einsum('ikh,jkh->ijh', a_full, b_full, precision=lax.Precision.HIGHEST)
    centered_scaled_input, inverse_deviation = apply_layer_norm(hidden_state)
    normalized_input = centered_scaled_input.astype(jnp.bfloat16)
    output = flat_dot(normalized_input, out_weight)
    gate = jax.nn.sigmoid(flat_dot(normed, gate_weight))
    upstream = cotangent.astype(jnp.float32)
    dgate = (upstream * output * gate * (1.0 - gate)).astype(jnp.bfloat16)
    dout = (upstream * gate).astype(jnp.bfloat16)
    normed_flat = normed.reshape(-1, C)
    gate_grad = jnp.dot(normed_flat.T, dgate.reshape(-1, C), preferred_element_type=jnp.float32) / N
    out_grad = jnp.dot(normalized_input.reshape(-1, H).T, dout.reshape(-1, C), preferred_element_type=jnp.float32) / N
    normalized_input_gradient = flat_dot(dout, out_weight.T)
    hidden_gradient = layer_norm_backward(normalized_input_gradient, centered_scaled_input, inverse_deviation).astype(jnp.bfloat16).astype(jnp.float32)
    grad_a = jnp.einsum('ijh,jkh->ikh', hidden_gradient, b_full, precision=lax.Precision.HIGHEST)
    grad_b = jnp.einsum('ijh,ikh->jkh', hidden_gradient, a_full, precision=lax.Precision.HIGHEST)
    dproj = jnp.concatenate([grad_a * sig_a, grad_a * a_val * sig_a * (1.0 - sig_a), grad_b * sig_b, grad_b * b_val * sig_b * (1.0 - sig_b)], axis=-1).astype(jnp.bfloat16)
    in_grad = jnp.dot(normed_flat.T, dproj.reshape(-1, 4 * H), preferred_element_type=jnp.float32) / N
    dnormed = flat_dot(dproj, in_weight.T) + flat_dot(dgate, gate_weight.T)
    pair_grad = layer_norm_backward(dnormed, zhat, zinv).astype(jnp.bfloat16)
    return (pair_grad, in_grad, gate_grad, out_grad)
```

```python
import jax
import jax.numpy as jnp
from jax import lax
from jax.sharding import Mesh, PartitionSpec as P

ROW = ("y", "zh")
CHI = ("zl", "x")
OWNERS = ("y", "zh", "zl", "x")
ALL = ("y", "zh", "zl", "x", "core")
SWAP = [(0, 1), (1, 0)]
BF = jnp.bfloat16
F32 = jnp.float32


def apply_layer_norm(values, axis):
    center = values - jnp.mean(values, axis=axis, keepdims=True)
    scale = lax.rsqrt(jnp.mean(center * center, axis=axis, keepdims=True) + 1e-05)
    return (center * scale, scale)


def layer_norm_backward(grad, normal, scale, axis):
    first = jnp.mean(grad, axis=axis, keepdims=True)
    second = jnp.mean(grad * normal, axis=axis, keepdims=True)
    return scale * (grad - first - normal * second)


def dot(left, right, contract):
    return lax.dot_general(left, right, (contract, ((), ())), preferred_element_type=F32)


def exchange(values, axes):
    return lax.all_to_all(values, axes, 0, 0, tiled=True)


def per_device(pair, cotangent, in_weight, gate_weight, out_weight):
    t = pair.shape[0]
    chans = pair.shape[2]
    hid = out_weight.shape[0]
    core = lax.axis_index("core")
    rows, chi = 16, 8
    total = t * rows
    tile = t * t
    zhat, zinv = apply_layer_norm(pair.astype(F32).reshape(tile, chans), -1)
    normed = zhat.astype(BF)
    proj = dot(in_weight, normed, ((0,), (1,)))
    a_val, sig_a = proj[0:hid], jax.nn.sigmoid(proj[hid : 2 * hid])
    b_val, sig_b = proj[2 * hid : 3 * hid], jax.nn.sigmoid(proj[3 * hid : 4 * hid])
    ab = jnp.concatenate([(sig_a * a_val).astype(BF), (sig_b * b_val).astype(BF)], axis=1)
    ab = exchange(ab.reshape(hid, 16, 128), OWNERS).reshape(rows, chi, 2, t, t)
    ab = jnp.transpose(ab, (2, 0, 3, 1, 4)).reshape(2, rows * t, chi * t)
    a_own, b_own = ab[0], ab[1]

    x = dot(a_own, b_own, ((1,), (1,))).reshape(rows * t, chi, 2, t)
    keep = lax.dynamic_index_in_dim(x, core, 2, keepdims=False)
    give = lax.dynamic_index_in_dim(x, 1 - core, 2, keepdims=False)
    x = (keep + lax.ppermute(give, "core", SWAP)).astype(BF)
    x = jnp.transpose(x.reshape(rows, t, chi, t), (0, 2, 1, 3)).reshape(hid, 8, 128)
    x = exchange(x, OWNERS).reshape(hid, tile).astype(F32)

    xhat, xinv = apply_layer_norm(x, 0)
    xnorm = xhat.astype(BF)
    gate = jax.nn.sigmoid(dot(normed, gate_weight, ((1,), (0,))))
    upstream = cotangent.astype(F32).reshape(tile, chans)
    dout = (upstream * gate).astype(BF)
    dxnorm = dot(out_weight, dout, ((1,), (1,)))
    dx = layer_norm_backward(dxnorm, xhat, xinv, 0).astype(BF)
    dx = exchange(dx.reshape(hid, 8, 128), OWNERS)
    other = lax.ppermute(dx, "core", SWAP)
    dx = jnp.stack([jnp.where(core == 0, dx, other), jnp.where(core == 0, other, dx)])
    dx = jnp.transpose(dx.reshape(2, rows, chi, t, t), (1, 3, 2, 0, 4)).reshape(rows * t, rows * t)

    da = dot(dx, b_own, ((1,), (0,)))
    db = dot(dx, a_own, ((0,), (0,)))
    dab = jnp.stack([da, db]).astype(BF).reshape(2, rows, t, chi, t)
    dab = jnp.transpose(dab, (1, 3, 0, 2, 4)).reshape(hid, 16, 128)
    dab = exchange(dab, OWNERS).reshape(hid, 2, tile).astype(F32)
    da, db = dab[:, 0], dab[:, 1]

    out = dot(xnorm, out_weight, ((0,), (0,)))
    dgate = (upstream * out * gate * (1.0 - gate)).astype(BF)
    dproj = jnp.concatenate(
        [
            da * sig_a,
            da * a_val * sig_a * (1.0 - sig_a),
            db * sig_b,
            db * b_val * sig_b * (1.0 - sig_b),
        ],
        axis=0,
    ).astype(BF)
    in_part = dot(normed, dproj, ((0,), (1,)))
    gate_part = dot(normed, dgate, ((0,), (0,)))
    out_part = dot(xnorm, dout, ((1,), (0,)))
    parts = jnp.concatenate([in_part.reshape(-1), gate_part.reshape(-1), out_part.reshape(-1)])
    parts = exchange(parts.reshape(256, -1, 128), ALL)
    share = jnp.sum(parts, axis=0, keepdims=True) / total
    whole = exchange(jnp.broadcast_to(share, (256,) + share.shape[1:]), ALL).reshape(-1)
    n_in, n_gate = chans * 4 * hid, chans * chans
    in_grad = whole[:n_in].reshape(chans, 4 * hid)
    gate_grad = whole[n_in : n_in + n_gate].reshape(chans, chans)
    out_grad = whole[n_in + n_gate :].reshape(hid, chans)

    dnormed = dot(dproj, in_weight, ((0,), (1,))) + dot(dgate, gate_weight, ((1,), (1,)))
    pair_grad = layer_norm_backward(dnormed, zhat, zinv, -1).astype(BF).reshape(t, t, chans)
    return (pair_grad, in_grad, gate_grad, out_grad)


def solution(mesh):
    fine = Mesh(mesh.devices.reshape(4, 4, 2, 4, 2), ALL)
    tiles = P(ROW, CHI + ("core",), None)
    return jax.shard_map(
        per_device,
        mesh=fine,
        in_specs=(tiles, tiles, P(), P(), P()),
        out_specs=(tiles, P(), P(), P()),
        check_vma=False,
    )
```

```python
import jax
import jax.numpy as jnp
from jax import lax
from jax.experimental import pallas as pl
from jax.experimental.pallas import tpu as pltpu
from jax.sharding import Mesh, PartitionSpec as P

ROW = ("y", "zh")
CHI = ("zl", "x")
OWNERS = ("y", "zh", "zl", "x")
PLANE = ("y", "x", "core")
LINE = ("zh", "zl")
ALL = ("y", "zh", "zl", "x", "core")
SWAP = [(0, 1), (1, 0)]
BF = jnp.bfloat16
F32 = jnp.float32
EPS = 1e-05


def dot(left, right, contract=((1,), (0,))):
    return lax.dot_general(left, right, (contract, ((), ())), preferred_element_type=F32)


def layer_norm(values, axis=-1):
    center = values - jnp.mean(values, axis=axis, keepdims=True)
    scale = lax.rsqrt(jnp.mean(center * center, axis=axis, keepdims=True) + EPS)
    return center * scale, scale


def layer_norm_backward(grad, normal, scale, axis=-1):
    first = jnp.mean(grad, axis=axis, keepdims=True)
    second = jnp.mean(grad * normal, axis=axis, keepdims=True)
    return scale * (grad - first - normal * second)


def regroup(parts):
    lane = lax.broadcasted_iota(jnp.int32, parts[0].shape, 1)
    low = lane < 64
    even = (lane // 32) % 2 == 0
    p0, p1, p2, p3 = parts
    roll = lambda v, n: pltpu.roll(v, n, 1)
    p0, p2 = jnp.where(low, p0, roll(p2, 64)), jnp.where(low, roll(p0, 64), p2)
    p1, p3 = jnp.where(low, p1, roll(p3, 64)), jnp.where(low, roll(p1, 64), p3)
    p0, p1 = jnp.where(even, p0, roll(p1, 32)), jnp.where(even, roll(p0, 96), p1)
    p2, p3 = jnp.where(even, p2, roll(p3, 32)), jnp.where(even, roll(p2, 96), p3)
    return [p0, p1, p2, p3]


def project_kernel(pair_ref, w_ref, msg_ref, held):
    w = w_ref[...]
    for s in range(8):
        zhat, _ = layer_norm(pair_ref[:, s].astype(F32).reshape(128, 128))
        proj = dot(w, zhat.astype(BF), ((0,), (1,)))
        held[pl.ds(s, 128, stride=16), :] = jax.nn.sigmoid(proj[128:256]) * proj[0:128]
        held[pl.ds(8 + s, 128, stride=16), :] = jax.nn.sigmoid(proj[384:512]) * proj[256:384]
    msg_ref[...] = held[...].reshape(128, 16, 128).astype(BF)


def side_kernel(pair_ref, cot_ref, w_ref, gw_ref, ow_ref, fac_ref, norm_ref, g2_ref, dout_ref, dxn_ref):
    w = w_ref[...]
    gw = gw_ref[...]
    ow = ow_ref[...]
    for s in range(8):
        zhat, _ = layer_norm(pair_ref[:, s].astype(F32).reshape(128, 128))
        normed = zhat.astype(BF)
        norm_ref[s] = normed
        proj = dot(w, normed, ((0,), (1,)))
        for n in range(2):
            val = proj[256 * n : 256 * n + 128]
            sig = jax.nn.sigmoid(proj[256 * n + 128 : 256 * n + 256])
            fac_ref[s, 256 * n : 256 * n + 128] = sig
            fac_ref[s, 256 * n + 128 : 256 * n + 256] = val * sig * (1.0 - sig)
        gate = jax.nn.sigmoid(dot(normed, gw))
        upstream = cot_ref[:, s].astype(F32).reshape(128, 128)
        dout = upstream * gate
        g2_ref[s] = dout * (1.0 - gate)
        dout = dout.astype(BF)
        dout_ref[s] = dout
        dxn_ref[pl.ds(s, 128, stride=8), :] = dot(ow, dout, ((1,), (1,)))


def pack_kernel(core_ref, msg_ref, a_ref, b_ref, give_ref):
    core = core_ref[0]
    for t in range(2):
        parts = [msg_ref[:, :, 4 * t + q].astype(F32)[:, :, 0:8].reshape(128, 128) for q in range(4)]
        for g, part in enumerate(regroup(parts)):
            a_ref[pl.ds(128 * g, 128), pl.ds(128 * t, 128)] = part.astype(BF)
        for half in range(2):
            sel = core if half == 0 else 1 - core
            parts = [msg_ref[:, sel, 4 * t + q].astype(F32)[:, 8:16].reshape(64, 128) for q in range(4)]
            parts = [part.reshape(8, 8, 128) for part in regroup(parts)]
            b_ref[half, :, pl.ds(128 * t, 128)] = jnp.stack(parts, axis=1).reshape(256, 128).astype(BF)
    give_ref[...] = dot(a_ref[...], b_ref[1], ((1,), (1,)))


def x_kernel(a_ref, b_ref, got_ref, msg_ref):
    x = dot(a_ref[...], b_ref[0], ((1,), (1,))) + got_ref[...]
    for t in range(2):
        parts = [x[128 * g : 128 * g + 128, 128 * t : 128 * t + 128] for g in range(4)]
        for q, part in enumerate(regroup(parts)):
            msg_ref[:, 4 * t + q] = part.reshape(16, 8, 128).astype(BF)


def dx_kernel(x_ref, dxn_ref, msg_ref, xhat_ref):
    xhat, xinv = layer_norm(x_ref[...].astype(F32), 0)
    xhat_ref[...] = xhat
    msg_ref[...] = layer_norm_backward(dxn_ref[...], xhat, xinv, 0).astype(BF)


def gate_kernel(xhat_ref, norm_ref, g2_ref, dout_ref, gw_ref, ow_ref, gate_ref, out_ref, dn_ref):
    gw = gw_ref[...]
    ow = ow_ref[...]
    gate_part = jnp.zeros((128, 128), F32)
    out_part = jnp.zeros((128, 128), F32)
    for s in range(8):
        xnorm = xhat_ref[pl.ds(s, 128, stride=8), :].astype(BF)
        dgate = (g2_ref[s] * dot(xnorm, ow, ((0,), (0,)))).astype(BF)
        gate_part += dot(norm_ref[s], dgate, ((0,), (0,)))
        out_part += dot(xnorm, dout_ref[s])
        dn_ref[s] = dot(dgate, gw, ((1,), (1,)))
    gate_ref[...] = gate_part
    out_ref[...] = out_part


def pull_kernel(core_ref, own_ref, other_ref, a_ref, b_ref, msg_ref, dx, held):
    core = core_ref[0]
    for half, ref in enumerate((own_ref, other_ref)):
        for t in range(2):
            parts = [ref[:, 4 * t + q].astype(F32).reshape(128, 128) for q in range(4)]
            for g, part in enumerate(regroup(parts)):
                dx[half, pl.ds(128 * g, 128), pl.ds(128 * t, 128)] = part.astype(BF)
    da = dot(dx[0], b_ref[0]) + dot(dx[1], b_ref[1])
    for t in range(2):
        parts = [da[128 * g : 128 * g + 128, 128 * t : 128 * t + 128] for g in range(4)]
        for q, part in enumerate(regroup(parts)):
            held[:, :, 4 * t + q, 0:8] = part.reshape(8, 2, 8, 128)
    for half in range(2):
        sel = core if half == 0 else 1 - core
        db = dot(dx[half], a_ref[...], ((0,), (0,))).reshape(8, 4, 8, 256)
        for t in range(2):
            parts = [db[:, g, :, 128 * t : 128 * t + 128].reshape(64, 128) for g in range(4)]
            for q, part in enumerate(regroup(parts)):
                held[:, sel, 4 * t + q, 8:16] = part.reshape(8, 8, 128)
    msg_ref[...] = held[...].astype(BF)


def weight_kernel(dab_ref, fac_ref, norm_ref, gate_ref, out_ref, sum_ref, dproj_ref, held):
    held[...] = dab_ref[...].astype(F32).reshape(2048, 128)
    total = jnp.zeros((512, 128), F32)
    for s in range(8):
        da = held[pl.ds(s, 128, stride=16), :]
        db = held[pl.ds(8 + s, 128, stride=16), :]
        fac = fac_ref[s]
        dproj = jnp.concatenate(
            [da * fac[0:128], da * fac[128:256], db * fac[256:384], db * fac[384:512]], axis=0
        ).astype(BF)
        dproj_ref[s] = dproj
        total += dot(dproj, norm_ref[s])
    sum_ref[0:512] = total
    sum_ref[512:640] = gate_ref[...]
    sum_ref[640:768] = out_ref[...]


def pair_kernel(dproj_ref, w_ref, dn_ref, pair_ref, out_ref):
    w = w_ref[...]
    for s in range(8):
        zhat, zinv = layer_norm(pair_ref[:, s].astype(F32).reshape(128, 128))
        dnormed = dot(dproj_ref[s], w, ((0,), (1,))) + dn_ref[s]
        grad = layer_norm_backward(dnormed, zhat, zinv)
        out_ref[:, s] = grad.reshape(4, 32, 128).astype(BF)


def run(kernel, outs, *args, scratch=(), scalars=0, flops=0):
    outs = [jax.ShapeDtypeStruct(shape, dtype) for shape, dtype in outs]
    vmem = pl.BlockSpec(memory_space=pltpu.VMEM)
    smem = pl.BlockSpec(memory_space=pltpu.SMEM)
    size = sum(v.size * v.dtype.itemsize for v in list(args) + outs)
    result = pl.pallas_call(
        kernel,
        out_shape=outs,
        in_specs=[smem] * scalars + [vmem] * (len(args) - scalars),
        out_specs=[vmem] * len(outs),
        scratch_shapes=scratch,
        compiler_params=pltpu.CompilerParams(vmem_limit_bytes=24 * 1024 * 1024),
        cost_estimate=pl.CostEstimate(flops=flops, bytes_accessed=size, transcendentals=0),
    )(*args)
    return result[0] if len(outs) == 1 else result


def exchange(values, axes):
    return lax.all_to_all(values, axes, 0, 0, tiled=True)


def per_device(pair, cotangent, in_weight, gate_weight, out_weight):
    core = jnp.reshape(lax.axis_index("core"), (1,)).astype(jnp.int32)
    total = 512
    pair = pair.reshape(4, 8, 32, 128)
    cotangent = cotangent.reshape(4, 8, 32, 128)

    msg = run(
        project_kernel, [((128, 16, 128), BF)], pair, in_weight,
        scratch=[pltpu.VMEM((2048, 128), F32)], flops=134_000_000,
    )
    msg = exchange(msg, OWNERS).reshape(8, 2, 8, 16, 128)
    factors, normed, g2, dout, dxnorm = run(
        side_kernel,
        [((8, 512, 128), F32), ((8, 128, 128), BF), ((8, 128, 128), F32), ((8, 128, 128), BF), ((1024, 128), F32)],
        pair, cotangent, in_weight, gate_weight, out_weight, flops=200_000_000,
    )
    a_own, b_own, give = run(
        pack_kernel, [((512, 256), BF), ((2, 256, 256), BF), ((512, 256), F32)],
        core, msg, scalars=1, flops=67_000_000,
    )
    got = lax.ppermute(give, "core", SWAP)
    x = run(x_kernel, [((16, 8, 8, 128), BF)], a_own, b_own, got, flops=67_000_000)
    x = exchange(x.reshape(128, 8, 128), OWNERS)
    dx, xhat = run(
        dx_kernel, [((128, 8, 128), BF), ((128, 8, 128), F32)], x, dxnorm.reshape(128, 8, 128), flops=1_000_000
    )
    own = exchange(dx, OWNERS)
    gate_part, out_part, dn_gate = run(
        gate_kernel,
        [((128, 128), F32), ((128, 128), F32), ((8, 128, 128), F32)],
        xhat.reshape(1024, 128), normed, g2, dout, gate_weight, out_weight, flops=134_000_000,
    )
    other = lax.ppermute(own, "core", SWAP)
    dab = run(
        pull_kernel, [((8, 2, 8, 16, 128), BF)],
        core, own.reshape(16, 8, 8, 128), other.reshape(16, 8, 8, 128), a_own, b_own,
        scratch=[pltpu.VMEM((2, 512, 256), BF), pltpu.VMEM((8, 2, 8, 16, 128), F32)], scalars=1, flops=268_000_000,
    )
    dab = exchange(dab.reshape(128, 16, 128), OWNERS)
    parts, dproj = run(
        weight_kernel, [((768, 128), F32), ((8, 512, 128), BF)],
        dab, factors, normed, gate_part, out_part, scratch=[pltpu.VMEM((2048, 128), F32)], flops=134_000_000,
    )
    parts = jnp.sum(exchange(parts.reshape(32, 24, 128), PLANE), axis=0, keepdims=True)
    pair_grad = run(
        pair_kernel, [((4, 8, 32, 128), BF)], dproj, in_weight, dn_gate, pair, flops=134_000_000
    )
    parts = jnp.sum(exchange(jnp.broadcast_to(parts, (8, 24, 128)), LINE), axis=0, keepdims=True) / total
    whole = exchange(jnp.broadcast_to(parts, (32, 24, 128)), PLANE).reshape(768, 128)
    return (pair_grad.reshape(32, 32, 128), whole[0:512].T, whole[512:640], whole[640:768])


def solution(mesh):
    fine = Mesh(mesh.devices.reshape(4, 4, 2, 4, 2), ALL)
    tiles = P(ROW, CHI + ("core",), None)
    return jax.shard_map(
        per_device,
        mesh=fine,
        in_specs=(tiles, tiles, P(), P(), P()),
        out_specs=(tiles, P(), P(), P()),
        check_vma=False,
    )
```

```python
import jax
import jax.numpy as jnp
from jax import lax
from jax.experimental import pallas as pl
from jax.experimental.pallas import tpu as pltpu
from jax.sharding import Mesh, PartitionSpec as P

ROW = ("y", "zh")
CHI = ("zl", "x")
OWNERS = ("zl", "y", "zh", "x")
PLANE = ("core", "y", "x")
LINE = ("zh", "zl")
ALL = ("y", "zh", "zl", "x", "core")
SWAP = [(0, 1), (1, 0)]
BF = jnp.bfloat16
F32 = jnp.float32
EPS = 1e-05


def dot(left, right, contract=((1,), (0,))):
    return lax.dot_general(left, right, (contract, ((), ())), preferred_element_type=F32)


def layer_norm(values, axis=-1):
    center = values - jnp.mean(values, axis=axis, keepdims=True)
    scale = lax.rsqrt(jnp.mean(center * center, axis=axis, keepdims=True) + EPS)
    return center * scale, scale


def layer_norm_backward(grad, normal, scale, axis=-1):
    first = jnp.mean(grad, axis=axis, keepdims=True)
    second = jnp.mean(grad * normal, axis=axis, keepdims=True)
    return scale * (grad - first - normal * second)


def regroup(parts):
    lane = lax.broadcasted_iota(jnp.int32, parts[0].shape, 1)
    low = lane < 64
    even = (lane // 32) % 2 == 0
    p0, p1, p2, p3 = parts
    roll = lambda v, n: pltpu.roll(v, n, 1)
    p0, p2 = jnp.where(low, p0, roll(p2, 64)), jnp.where(low, roll(p0, 64), p2)
    p1, p3 = jnp.where(low, p1, roll(p3, 64)), jnp.where(low, roll(p1, 64), p3)
    p0, p1 = jnp.where(even, p0, roll(p1, 32)), jnp.where(even, roll(p0, 96), p1)
    p2, p3 = jnp.where(even, p2, roll(p3, 32)), jnp.where(even, roll(p2, 96), p3)
    return [p0, p1, p2, p3]


def project_kernel(pair_ref, w_ref, msg_ref, norm_ref, held):
    w = w_ref[...]
    for s in range(8):
        zhat, _ = layer_norm(pair_ref[:, s].astype(F32).reshape(128, 128))
        normed = zhat.astype(BF)
        norm_ref[s] = normed
        proj = dot(w, normed, ((0,), (1,)))
        held[pl.ds(s, 128, stride=16), :] = jax.nn.sigmoid(proj[128:256]) * proj[0:128]
        held[pl.ds(8 + s, 128, stride=16), :] = jax.nn.sigmoid(proj[384:512]) * proj[256:384]
    msg_ref[...] = held[...].reshape(128, 16, 128).astype(BF)


def side_kernel(norm_ref, cot_ref, gw_ref, ow_ref, g2_ref, dout_ref, dxn_ref):
    gw = gw_ref[...]
    ow = ow_ref[...]
    for s in range(8):
        gate = jax.nn.sigmoid(dot(norm_ref[s], gw))
        upstream = cot_ref[:, s].astype(F32).reshape(128, 128)
        dout = upstream * gate
        g2_ref[s] = dout * (1.0 - gate)
        dout = dout.astype(BF)
        dout_ref[s] = dout
        dxn_ref[pl.ds(s, 128, stride=8), :] = dot(ow, dout, ((1,), (1,)))


def pack_kernel(core_ref, msg_ref, a_ref, b_ref, give_ref):
    core = core_ref[0]
    for t in range(2):
        parts = [msg_ref[t, :, :, q].astype(F32)[:, :, 0:8].reshape(128, 128) for q in range(4)]
        for g, part in enumerate(regroup(parts)):
            a_ref[pl.ds(128 * g, 128), pl.ds(128 * t, 128)] = part.astype(BF)
        for half in range(2):
            sel = core if half == 0 else 1 - core
            parts = [msg_ref[t, :, sel, q].astype(F32)[:, 8:16].reshape(64, 128) for q in range(4)]
            parts = [part.reshape(8, 8, 128) for part in regroup(parts)]
            b_ref[half, :, pl.ds(128 * t, 128)] = jnp.stack(parts, axis=1).reshape(256, 128).astype(BF)
    give_ref[...] = dot(a_ref[...], b_ref[1], ((1,), (1,)))


def x_kernel(a_ref, b_ref, got_ref, msg_ref):
    x = dot(a_ref[...], b_ref[0], ((1,), (1,))) + got_ref[...]
    for t in range(2):
        parts = [x[128 * g : 128 * g + 128, 128 * t : 128 * t + 128] for g in range(4)]
        for q, part in enumerate(regroup(parts)):
            msg_ref[t, :, q] = part.reshape(16, 8, 128).astype(BF)


def dx_kernel(x_ref, dxn_ref, msg_ref, xhat_ref):
    xhat, xinv = layer_norm(x_ref[...].astype(F32), 0)
    xhat_ref[...] = xhat
    msg_ref[...] = layer_norm_backward(dxn_ref[...], xhat, xinv, 0).astype(BF)


def late_kernel(xhat_ref, norm_ref, g2_ref, dout_ref, w_ref, gw_ref, ow_ref, sum_ref, dn_ref, fac_ref):
    w = w_ref[...]
    gw = gw_ref[...]
    ow = ow_ref[...]
    gate_part = jnp.zeros((128, 128), F32)
    out_part = jnp.zeros((128, 128), F32)
    for s in range(8):
        normed = norm_ref[s]
        xnorm = xhat_ref[pl.ds(s, 128, stride=8), :].astype(BF)
        dgate = (g2_ref[s] * dot(xnorm, ow, ((0,), (0,)))).astype(BF)
        gate_part += dot(normed, dgate, ((0,), (0,)))
        out_part += dot(xnorm, dout_ref[s])
        dn_ref[s] = dot(dgate, gw, ((1,), (1,)))
        proj = dot(w, normed, ((0,), (1,)))
        for n in range(2):
            val = proj[256 * n : 256 * n + 128]
            sig = jax.nn.sigmoid(proj[256 * n + 128 : 256 * n + 256])
            fac_ref[s, 256 * n : 256 * n + 128] = sig
            fac_ref[s, 256 * n + 128 : 256 * n + 256] = val * sig * (1.0 - sig)
    sum_ref[0:128] = gate_part
    sum_ref[128:256] = out_part


def pull_kernel(core_ref, own_ref, other_ref, a_ref, b_ref, msg_ref, dx, held):
    core = core_ref[0]
    for half, ref in enumerate((own_ref, other_ref)):
        for t in range(2):
            parts = [ref[t, :, q].astype(F32).reshape(128, 128) for q in range(4)]
            for g, part in enumerate(regroup(parts)):
                dx[half, pl.ds(128 * g, 128), pl.ds(128 * t, 128)] = part.astype(BF)
    da = dot(dx[0], b_ref[0]) + dot(dx[1], b_ref[1])
    for t in range(2):
        parts = [da[128 * g : 128 * g + 128, 128 * t : 128 * t + 128] for g in range(4)]
        for q, part in enumerate(regroup(parts)):
            held[t, :, :, q, 0:8] = part.reshape(8, 2, 8, 128)
    for half in range(2):
        sel = core if half == 0 else 1 - core
        db = dot(dx[half], a_ref[...], ((0,), (0,))).reshape(8, 4, 8, 256)
        for t in range(2):
            parts = [db[:, g, :, 128 * t : 128 * t + 128].reshape(64, 128) for g in range(4)]
            for q, part in enumerate(regroup(parts)):
                held[t, :, sel, q, 8:16] = part.reshape(8, 8, 128)
    msg_ref[...] = held[...].astype(BF)


def weight_kernel(dab_ref, fac_ref, norm_ref, gate_out_ref, sum_ref, dproj_ref, held):
    held[...] = dab_ref[...].astype(F32).reshape(2048, 128)
    total = jnp.zeros((512, 128), F32)
    for s in range(8):
        da = held[pl.ds(s, 128, stride=16), :]
        db = held[pl.ds(8 + s, 128, stride=16), :]
        fac = fac_ref[s]
        dproj = jnp.concatenate(
            [da * fac[0:128], da * fac[128:256], db * fac[256:384], db * fac[384:512]], axis=0
        ).astype(BF)
        dproj_ref[s] = dproj
        total += dot(dproj, norm_ref[s])
    sum_ref[0:512] = total.astype(BF)
    sum_ref[512:768] = gate_out_ref[...].astype(BF)


def pair_kernel(dproj_ref, w_ref, dn_ref, pair_ref, out_ref):
    w = w_ref[...]
    for s in range(8):
        zhat, zinv = layer_norm(pair_ref[:, s].astype(F32).reshape(128, 128))
        dnormed = dot(dproj_ref[s], w, ((0,), (1,))) + dn_ref[s]
        grad = layer_norm_backward(dnormed, zhat, zinv)
        out_ref[:, s] = grad.reshape(4, 32, 128).astype(BF)


def collect_kernel(rows_ref, in_ref, gate_ref, out_ref):
    in_ref[...] = rows_ref[0:512].astype(F32).T
    gate_ref[...] = rows_ref[512:640].astype(F32)
    out_ref[...] = rows_ref[640:768].astype(F32)


def run(kernel, outs, *args, scratch=(), scalars=0, flops=0):
    outs = [jax.ShapeDtypeStruct(shape, dtype) for shape, dtype in outs]
    vmem = pl.BlockSpec(memory_space=pltpu.VMEM)
    smem = pl.BlockSpec(memory_space=pltpu.SMEM)
    size = sum(v.size * v.dtype.itemsize for v in list(args) + outs)
    result = pl.pallas_call(
        kernel,
        out_shape=outs,
        in_specs=[smem] * scalars + [vmem] * (len(args) - scalars),
        out_specs=[vmem] * len(outs),
        scratch_shapes=scratch,
        compiler_params=pltpu.CompilerParams(vmem_limit_bytes=16 * 1024 * 1024),
        cost_estimate=pl.CostEstimate(flops=flops, bytes_accessed=size, transcendentals=0),
    )(*args)
    return result[0] if len(outs) == 1 else result


def exchange(values, axes):
    return lax.all_to_all(values, axes, 0, 0, tiled=True)


def per_device(pair, cotangent, in_weight, gate_weight, out_weight):
    core = jnp.reshape(lax.axis_index("core"), (1,)).astype(jnp.int32)
    total = 512
    pair = pair.reshape(4, 8, 32, 128)
    cotangent = cotangent.reshape(4, 8, 32, 128)

    msg, normed = run(
        project_kernel, [((128, 16, 128), BF), ((8, 128, 128), BF)], pair, in_weight,
        scratch=[pltpu.VMEM((2048, 128), F32)], flops=134_000_000,
    )
    msg = exchange(msg, OWNERS).reshape(2, 8, 2, 4, 16, 128)
    g2, dout, dxnorm = run(
        side_kernel, [((8, 128, 128), F32), ((8, 128, 128), BF), ((1024, 128), F32)],
        normed, cotangent, gate_weight, out_weight, flops=67_000_000,
    )
    a_own, b_own, give = run(
        pack_kernel, [((512, 256), BF), ((2, 256, 256), BF), ((512, 256), F32)],
        core, msg, scalars=1, flops=67_000_000,
    )
    got = lax.ppermute(give, "core", SWAP)
    x = run(x_kernel, [((2, 16, 4, 8, 128), BF)], a_own, b_own, got, flops=67_000_000)
    x = exchange(x.reshape(128, 8, 128), OWNERS)
    dx, xhat = run(
        dx_kernel, [((128, 8, 128), BF), ((128, 8, 128), F32)], x, dxnorm.reshape(128, 8, 128), flops=1_000_000
    )
    own = exchange(dx, OWNERS)
    sums, dn_gate, factors = run(
        late_kernel, [((256, 128), F32), ((8, 128, 128), F32), ((8, 512, 128), F32)],
        xhat.reshape(1024, 128), normed, g2, dout, in_weight, gate_weight, out_weight, flops=268_000_000,
    )
    other = lax.ppermute(own, "core", SWAP)
    dab = run(
        pull_kernel, [((2, 8, 2, 4, 16, 128), BF)],
        core, own.reshape(2, 16, 4, 8, 128), other.reshape(2, 16, 4, 8, 128), a_own, b_own,
        scratch=[pltpu.VMEM((2, 512, 256), BF), pltpu.VMEM((2, 8, 2, 4, 16, 128), F32)], scalars=1, flops=268_000_000,
    )
    dab = exchange(dab.reshape(128, 16, 128), OWNERS)
    parts, dproj = run(
        weight_kernel, [((768, 128), BF), ((8, 512, 128), BF)],
        dab, factors, normed, sums, scratch=[pltpu.VMEM((2048, 128), F32)], flops=134_000_000,
    )
    parts = exchange(parts.reshape(32, 24, 128), PLANE).astype(F32)
    parts = jnp.sum(parts, axis=0, keepdims=True).astype(BF)
    parts = exchange(jnp.broadcast_to(parts, (8, 24, 128)), LINE).astype(F32)
    parts = (jnp.sum(parts, axis=0, keepdims=True) / total).astype(BF)
    whole = exchange(jnp.broadcast_to(parts, (32, 24, 128)), PLANE).reshape(768, 128)
    pair_grad = run(
        pair_kernel, [((4, 8, 32, 128), BF)], dproj, in_weight, dn_gate, pair, flops=134_000_000
    )
    in_grad, gate_grad, out_grad = run(
        collect_kernel, [((128, 512), F32), ((128, 128), F32), ((128, 128), F32)], whole
    )
    return (pair_grad.reshape(32, 32, 128), in_grad, gate_grad, out_grad)


def solution(mesh):
    fine = Mesh(mesh.devices.reshape(4, 4, 2, 4, 2), ALL)
    tiles = P(ROW, CHI + ("core",), None)
    return jax.shard_map(
        per_device,
        mesh=fine,
        in_specs=(tiles, tiles, P(), P(), P()),
        out_specs=(tiles, P(), P(), P()),
        check_vma=False,
    )
```

```python
import functools

import jax
import jax.numpy as jnp
from jax import lax
from jax.experimental import pallas as pl
from jax.experimental.pallas import tpu as pltpu
from jax.sharding import Mesh, PartitionSpec as P

ROW = ("y", "zh")
CHI = ("zl", "x")
OWNERS = ("zl", "y", "zh", "x")
PLANE = ("core", "y", "x")
LINE = ("zh", "zl")
ALL = ("y", "zh", "zl", "x", "core")
SWAP = [(0, 1), (1, 0)]
BF = jnp.bfloat16
F32 = jnp.float32
EPS = 1e-05


def dot(left, right, contract=((1,), (0,))):
    return lax.dot_general(left, right, (contract, ((), ())), preferred_element_type=F32)


def layer_norm(values, axis=-1):
    center = values - jnp.mean(values, axis=axis, keepdims=True)
    scale = lax.rsqrt(jnp.mean(center * center, axis=axis, keepdims=True) + EPS)
    return center * scale, scale


def layer_norm_backward(grad, normal, scale, axis=-1):
    first = jnp.mean(grad, axis=axis, keepdims=True)
    second = jnp.mean(grad * normal, axis=axis, keepdims=True)
    return scale * (grad - first - normal * second)


def regroup(parts):
    lane = lax.broadcasted_iota(jnp.int32, parts[0].shape, 1)
    low = lane < 64
    even = (lane // 32) % 2 == 0
    p0, p1, p2, p3 = parts
    roll = lambda v, n: pltpu.roll(v, n, 1)
    p0, p2 = jnp.where(low, p0, roll(p2, 64)), jnp.where(low, roll(p0, 64), p2)
    p1, p3 = jnp.where(low, p1, roll(p3, 64)), jnp.where(low, roll(p1, 64), p3)
    p0, p1 = jnp.where(even, p0, roll(p1, 32)), jnp.where(even, roll(p0, 96), p1)
    p2, p3 = jnp.where(even, p2, roll(p3, 32)), jnp.where(even, roll(p2, 96), p3)
    return [p0, p1, p2, p3]


def project_kernel(pair_hbm, w_hbm, msg_ref, norm_ref, pair_ref, w_ref, held, sems):
    copies = [
        pltpu.make_async_copy(pair_hbm, pair_ref, sems.at[0]),
        pltpu.make_async_copy(w_hbm, w_ref, sems.at[1]),
    ]
    for copy in copies:
        copy.start()
    for copy in copies:
        copy.wait()
    w = w_ref[...]
    for s in range(8):
        zhat, _ = layer_norm(pair_ref[:, s].astype(F32).reshape(128, 128))
        normed = zhat.astype(BF)
        norm_ref[s] = normed
        proj = dot(w, normed, ((0,), (1,)))
        held[pl.ds(s, 128, stride=16), :] = jax.nn.sigmoid(proj[128:256]) * proj[0:128]
        held[pl.ds(8 + s, 128, stride=16), :] = jax.nn.sigmoid(proj[384:512]) * proj[256:384]
    msg_ref[...] = held[...].reshape(128, 16, 128).astype(BF)


def side_kernel(norm_ref, cot_ref, gw_ref, ow_ref, g2_ref, dout_ref, dxn_ref):
    gw = gw_ref[...]
    ow = ow_ref[...]
    for s in range(8):
        gate = jax.nn.sigmoid(dot(norm_ref[s], gw))
        upstream = cot_ref[:, s].astype(F32).reshape(128, 128)
        dout = upstream * gate
        g2_ref[s] = dout * (1.0 - gate)
        dout = dout.astype(BF)
        dout_ref[s] = dout
        dxn_ref[pl.ds(s, 128, stride=8), :] = dot(ow, dout, ((1,), (1,)))


def pack_kernel(core_ref, msg_ref, a_ref, b_ref, give_ref):
    core = core_ref[0]
    for t in range(2):
        parts = [msg_ref[t, :, :, q].astype(F32)[:, :, 0:8].reshape(128, 128) for q in range(4)]
        for g, part in enumerate(regroup(parts)):
            a_ref[pl.ds(128 * g, 128), pl.ds(128 * t, 128)] = part.astype(BF)
        for half in range(2):
            parts = [msg_ref[t, :, half, q].astype(F32)[:, 8:16].reshape(64, 128) for q in range(4)]
            parts = [part.reshape(8, 8, 128) for part in regroup(parts)]
            b_ref[half, :, pl.ds(128 * t, 128)] = jnp.stack(parts, axis=1).reshape(256, 128).astype(BF)
    to_message(dot(a_ref[...], b_ref[1 - core], ((1,), (1,))), give_ref)


def to_message(x, out_ref):
    for t in range(2):
        parts = [x[128 * g : 128 * g + 128, 128 * t : 128 * t + 128] for g in range(4)]
        for q, part in enumerate(regroup(parts)):
            out_ref[t, :, q] = part.reshape(16, 8, 128)


def keep_kernel(core_ref, a_ref, b_ref, keep_ref):
    to_message(dot(a_ref[...], b_ref[core_ref[0]], ((1,), (1,))), keep_ref)


def add_kernel(keep_ref, got_ref, msg_ref):
    msg_ref[...] = (keep_ref[...] + got_ref[...]).astype(BF)


def dx_kernel(x_ref, dxn_ref, msg_ref, xhat_ref):
    xhat, xinv = layer_norm(x_ref[...].astype(F32), 0)
    xhat_ref[...] = xhat
    msg_ref[...] = layer_norm_backward(dxn_ref[...], xhat, xinv, 0).astype(BF)


def late_kernel(xhat_ref, norm_ref, g2_ref, dout_ref, w_ref, gw_ref, ow_ref, sum_ref, dn_ref, fac_ref):
    w = w_ref[...]
    gw = gw_ref[...]
    ow = ow_ref[...]
    gate_part = jnp.zeros((128, 128), F32)
    out_part = jnp.zeros((128, 128), F32)
    for s in range(8):
        normed = norm_ref[s]
        xnorm = xhat_ref[pl.ds(s, 128, stride=8), :].astype(BF)
        dgate = (g2_ref[s] * dot(xnorm, ow, ((0,), (0,)))).astype(BF)
        gate_part += dot(normed, dgate, ((0,), (0,)))
        out_part += dot(xnorm, dout_ref[s])
        dn_ref[s] = dot(dgate, gw, ((1,), (1,)))
        proj = dot(w, normed, ((0,), (1,)))
        for n in range(2):
            val = proj[256 * n : 256 * n + 128]
            sig = jax.nn.sigmoid(proj[256 * n + 128 : 256 * n + 256])
            fac_ref[s, 256 * n : 256 * n + 128] = sig
            fac_ref[s, 256 * n + 128 : 256 * n + 256] = val * sig * (1.0 - sig)
    sum_ref[0:128] = gate_part.astype(BF)
    sum_ref[128:256] = out_part.astype(BF)


def pull_kernel(core_ref, own_ref, other_ref, a_ref, b_ref, msg_ref, dx, held):
    for n, ref in enumerate((own_ref, other_ref)):
        half = core_ref[0] if n == 0 else 1 - core_ref[0]
        for t in range(2):
            parts = [ref[t, :, q].astype(F32).reshape(128, 128) for q in range(4)]
            for g, part in enumerate(regroup(parts)):
                dx[half, pl.ds(128 * g, 128), pl.ds(128 * t, 128)] = part.astype(BF)
    da = dot(dx[0], b_ref[0]) + dot(dx[1], b_ref[1])
    for t in range(2):
        parts = [da[128 * g : 128 * g + 128, 128 * t : 128 * t + 128] for g in range(4)]
        for q, part in enumerate(regroup(parts)):
            held[t, :, :, q, 0:8] = part.reshape(8, 2, 8, 128)
    for half in range(2):
        db = dot(dx[half], a_ref[...], ((0,), (0,))).reshape(8, 4, 8, 256)
        for t in range(2):
            parts = [db[:, g, :, 128 * t : 128 * t + 128].reshape(64, 128) for g in range(4)]
            for q, part in enumerate(regroup(parts)):
                held[t, :, half, q, 8:16] = part.reshape(8, 8, 128)
    msg_ref[...] = held[...].astype(BF)


def weight_kernel(go_hbm, dab_ref, fac_ref, norm_ref, sum_hbm, dproj_ref, held, sums, sems):
    first = pltpu.make_async_copy(go_hbm, sum_hbm.at[pl.ds(512, 256)], sems.at[0])
    first.start()
    held[...] = dab_ref[...].astype(F32).reshape(2048, 128)
    total = jnp.zeros((512, 128), F32)
    for s in range(8):
        da = held[pl.ds(s, 128, stride=16), :]
        db = held[pl.ds(8 + s, 128, stride=16), :]
        fac = fac_ref[s]
        dproj = jnp.concatenate(
            [da * fac[0:128], da * fac[128:256], db * fac[256:384], db * fac[384:512]], axis=0
        ).astype(BF)
        dproj_ref[s] = dproj
        total += dot(dproj, norm_ref[s])
    sums[...] = total.astype(BF)
    last = pltpu.make_async_copy(sums, sum_hbm.at[pl.ds(0, 512)], sems.at[1])
    last.start()
    first.wait()
    last.wait()


def pair_kernel(dproj_ref, w_ref, dn_ref, pair_ref, out_ref):
    w = w_ref[...]
    for s in range(8):
        zhat, zinv = layer_norm(pair_ref[:, s].astype(F32).reshape(128, 128))
        dnormed = dot(dproj_ref[s], w, ((0,), (1,))) + dn_ref[s]
        grad = layer_norm_backward(dnormed, zhat, zinv)
        out_ref[:, s] = grad.reshape(4, 32, 128).astype(BF)


def sum_kernel(scale, parts_ref, out_ref):
    total = jnp.sum(parts_ref[...].astype(F32), axis=0, keepdims=True) * scale
    out_ref[...] = jnp.broadcast_to(total, out_ref.shape).astype(BF)


def collect_kernel(rows_ref, in_ref, gate_ref, out_ref):
    in_ref[...] = rows_ref[0:512].astype(F32).T
    gate_ref[...] = rows_ref[512:640].astype(F32)
    out_ref[...] = rows_ref[640:768].astype(F32)


def run(kernel, outs, *args, scratch=(), scalars=0, hbm=0, hbm_out=0, flops=0, after=(), grant=16):
    outs = [jax.ShapeDtypeStruct(shape, dtype) for shape, dtype in outs]
    vmem = pl.BlockSpec(memory_space=pltpu.VMEM)
    smem = pl.BlockSpec(memory_space=pltpu.SMEM)
    anywhere = pl.BlockSpec(memory_space=pltpu.HBM)
    skip = len(after)
    size = sum(v.size * v.dtype.itemsize for v in list(args) + outs)
    result = pl.pallas_call(
        lambda *refs: kernel(*refs[skip:]),
        out_shape=outs,
        in_specs=[anywhere] * (skip + hbm) + [smem] * scalars + [vmem] * (len(args) - scalars - hbm),
        out_specs=[anywhere] * hbm_out + [vmem] * (len(outs) - hbm_out),
        scratch_shapes=scratch,
        compiler_params=pltpu.CompilerParams(vmem_limit_bytes=grant * 1024 * 1024),
        cost_estimate=pl.CostEstimate(flops=flops, bytes_accessed=size, transcendentals=0),
    )(*after, *args)
    return result[0] if len(outs) == 1 else result


def exchange(values, axes):
    return lax.all_to_all(values, axes, 0, 0, tiled=True)


def per_device(pair, cotangent, in_weight, gate_weight, out_weight):
    core = jnp.reshape(lax.axis_index("core"), (1,)).astype(jnp.int32)
    pair = pair.reshape(4, 8, 32, 128)
    cotangent = cotangent.reshape(4, 8, 32, 128)

    msg, normed = run(
        project_kernel, [((128, 16, 128), BF), ((8, 128, 128), BF)], pair, in_weight, hbm=2, grant=56,
        scratch=[
            pltpu.VMEM((4, 8, 32, 128), BF), pltpu.VMEM((128, 512), BF),
            pltpu.VMEM((2048, 128), F32), pltpu.SemaphoreType.DMA((2,)),
        ],
        flops=134_000_000,
    )
    msg = exchange(msg, OWNERS).reshape(2, 8, 2, 4, 16, 128)
    g2, dout, dxnorm = run(
        side_kernel, [((8, 128, 128), F32), ((8, 128, 128), BF), ((1024, 128), F32)],
        normed, cotangent, gate_weight, out_weight, flops=67_000_000,
    )
    half = (2, 16, 4, 8, 128)
    a_own, b_own, give = run(
        pack_kernel, [((512, 256), BF), ((2, 256, 256), BF), (half, F32)],
        core, msg, scalars=1, flops=67_000_000,
    )
    got = lax.ppermute(give, "core", SWAP)
    keep = run(keep_kernel, [(half, F32)], core, a_own, b_own, scalars=1, flops=67_000_000)
    x = run(add_kernel, [(half, BF)], keep, got)
    x = exchange(x.reshape(128, 8, 128), OWNERS)
    dx, xhat = run(
        dx_kernel, [((128, 8, 128), BF), ((128, 8, 128), F32)], x, dxnorm.reshape(128, 8, 128), flops=1_000_000
    )
    dx = exchange(dx, OWNERS)
    dx = dx.reshape(2, 16, 4, 8, 128)
    other = lax.ppermute(dx, "core", SWAP)
    sums, dn_gate, factors = run(
        late_kernel, [((256, 128), BF), ((8, 128, 128), F32), ((8, 512, 128), F32)],
        xhat.reshape(1024, 128), normed, g2, dout, in_weight, gate_weight, out_weight, flops=268_000_000,
    )
    dab = run(
        pull_kernel, [((2, 8, 2, 4, 16, 128), BF)], core, dx, other, a_own, b_own, scalars=1, after=(dn_gate,),
        scratch=[pltpu.VMEM((2, 512, 256), BF), pltpu.VMEM((2, 8, 2, 4, 16, 128), F32)], flops=268_000_000,
    )
    dab = exchange(dab.reshape(128, 16, 128), OWNERS)
    parts, dproj = run(
        weight_kernel, [((768, 128), BF), ((8, 512, 128), BF)],
        sums, dab, factors, normed, hbm=1, hbm_out=1,
        scratch=[
            pltpu.VMEM((2048, 128), F32), pltpu.VMEM((512, 128), BF), pltpu.SemaphoreType.DMA((2,)),
        ],
        flops=134_000_000,
    )
    parts = exchange(parts.reshape(32, 24, 128), PLANE)
    pair_grad = run(
        pair_kernel, [((4, 8, 32, 128), BF)], dproj, in_weight, dn_gate, pair, flops=134_000_000
    )
    parts = run(functools.partial(sum_kernel, 1.0), [((8, 24, 128), BF)], parts, after=(pair_grad,))
    parts = exchange(parts, LINE)
    parts = run(functools.partial(sum_kernel, 1.0 / 512), [((32, 24, 128), BF)], parts)
    whole = exchange(parts, PLANE).reshape(768, 128)
    in_grad, gate_grad, out_grad = run(
        collect_kernel, [((128, 512), F32), ((128, 128), F32), ((128, 128), F32)], whole
    )
    return (pair_grad.reshape(32, 32, 128), in_grad, gate_grad, out_grad)


def solution(mesh):
    fine = Mesh(mesh.devices.reshape(4, 4, 2, 4, 2), ALL)
    tiles = P(ROW, CHI + ("core",), None)
    return jax.shard_map(
        per_device,
        mesh=fine,
        in_specs=(tiles, tiles, P(), P(), P()),
        out_specs=(tiles, P(), P(), P()),
        check_vma=False,
    )
```

```python
import functools

import jax
import jax.numpy as jnp
from jax import lax
from jax.experimental import pallas as pl
from jax.experimental.pallas import tpu as pltpu
from jax.sharding import Mesh, PartitionSpec as P

ROW = ("y", "zh")
CHI = ("zl", "x")
OWNERS = ("zl", "y", "zh", "x")
PLANE = ("core", "y", "x")
LINE = ("zh", "zl")
ALL = ("y", "zh", "zl", "x", "core")
SWAP = [(0, 1), (1, 0)]
BF = jnp.bfloat16
F32 = jnp.float32
EPS = 1e-05


def dot(left, right, contract=((1,), (0,))):
    return lax.dot_general(left, right, (contract, ((), ())), preferred_element_type=F32)


def layer_norm(values, axis=-1):
    center = values - jnp.mean(values, axis=axis, keepdims=True)
    scale = lax.rsqrt(jnp.mean(center * center, axis=axis, keepdims=True) + EPS)
    return center * scale, scale


def layer_norm_backward(grad, normal, scale, axis=-1):
    first = jnp.mean(grad, axis=axis, keepdims=True)
    second = jnp.mean(grad * normal, axis=axis, keepdims=True)
    return scale * (grad - first - normal * second)


def regroup(parts):
    lane = lax.broadcasted_iota(jnp.int32, parts[0].shape, 1)
    low = lane < 64
    even = (lane // 32) % 2 == 0
    p0, p1, p2, p3 = parts
    roll = lambda v, n: pltpu.roll(v, n, 1)
    p0, p2 = jnp.where(low, p0, roll(p2, 64)), jnp.where(low, roll(p0, 64), p2)
    p1, p3 = jnp.where(low, p1, roll(p3, 64)), jnp.where(low, roll(p1, 64), p3)
    p0, p1 = jnp.where(even, p0, roll(p1, 32)), jnp.where(even, roll(p0, 96), p1)
    p2, p3 = jnp.where(even, p2, roll(p3, 32)), jnp.where(even, roll(p2, 96), p3)
    return [p0, p1, p2, p3]


def project_kernel(pair_hbm, w_hbm, msg_ref, norm_ref, pair_ref, w_ref, held, sems):
    copies = [
        pltpu.make_async_copy(pair_hbm, pair_ref, sems.at[0]),
        pltpu.make_async_copy(w_hbm, w_ref, sems.at[1]),
    ]
    for copy in copies:
        copy.start()
    for copy in copies:
        copy.wait()
    w = w_ref[...]
    pair = jnp.concatenate([pair_ref[:, s].astype(F32).reshape(128, 128) for s in range(8)], axis=0)
    normed = layer_norm(pair)[0].astype(BF)
    norm_ref[...] = normed.reshape(8, 128, 128)
    for n in range(2):
        val = dot(w[:, 256 * n : 256 * n + 128], normed, ((0,), (1,)))
        sig = jax.nn.sigmoid(dot(w[:, 256 * n + 128 : 256 * n + 256], normed, ((0,), (1,))))
        val = val * sig
        for s in range(8):
            held[pl.ds(8 * n + s, 128, stride=16), :] = val[:, 128 * s : 128 * s + 128]
    msg_ref[...] = held[...].reshape(128, 16, 128).astype(BF)


def side_kernel(norm_ref, cot_ref, gw_ref, ow_ref, g2_ref, dout_ref, dxn_ref):
    gw = gw_ref[...]
    ow = ow_ref[...]
    for s in range(8):
        gate = jax.nn.sigmoid(dot(norm_ref[s], gw))
        upstream = cot_ref[:, s].astype(F32).reshape(128, 128)
        dout = upstream * gate
        g2_ref[s] = dout * (1.0 - gate)
        dout = dout.astype(BF)
        dout_ref[s] = dout
        dxn_ref[pl.ds(s, 128, stride=8), :] = dot(ow, dout, ((1,), (1,)))


def pack_kernel(core_ref, msg_ref, a_ref, b_ref, give_ref):
    core = core_ref[0]
    for t in range(2):
        parts = [msg_ref[t, :, :, q].astype(F32)[:, :, 0:8].reshape(128, 128) for q in range(4)]
        for g, part in enumerate(regroup(parts)):
            a_ref[pl.ds(128 * g, 128), pl.ds(128 * t, 128)] = part.astype(BF)
        for half in range(2):
            parts = [msg_ref[t, :, half, q].astype(F32)[:, 8:16].reshape(64, 128) for q in range(4)]
            parts = [part.reshape(8, 8, 128) for part in regroup(parts)]
            b_ref[half, :, pl.ds(128 * t, 128)] = jnp.stack(parts, axis=1).reshape(256, 128).astype(BF)
    to_message(dot(a_ref[...], b_ref[1 - core], ((1,), (1,))), give_ref)


def to_message(x, out_ref):
    for t in range(2):
        parts = [x[128 * g : 128 * g + 128, 128 * t : 128 * t + 128] for g in range(4)]
        for q, part in enumerate(regroup(parts)):
            out_ref[t, :, q] = part.reshape(16, 8, 128)


def keep_kernel(core_ref, a_ref, b_ref, keep_ref):
    to_message(dot(a_ref[...], b_ref[core_ref[0]], ((1,), (1,))), keep_ref)


def add_kernel(keep_ref, got_ref, msg_ref):
    msg_ref[...] = (keep_ref[...] + got_ref[...]).astype(BF)


def dx_kernel(x_ref, dxn_ref, msg_ref, xhat_ref):
    xhat, xinv = layer_norm(x_ref[...].astype(F32), 0)
    xhat_ref[...] = xhat
    msg_ref[...] = layer_norm_backward(dxn_ref[...], xhat, xinv, 0).astype(BF)


def late_kernel(xhat_ref, norm_ref, g2_ref, dout_ref, w_ref, ow_ref, sum_ref, dgate_ref, fac_ref):
    w = w_ref[...]
    ow = ow_ref[...]
    gate_part = jnp.zeros((128, 128), F32)
    out_part = jnp.zeros((128, 128), F32)
    for s in range(8):
        normed = norm_ref[s]
        xnorm = xhat_ref[pl.ds(s, 128, stride=8), :].astype(BF)
        dgate = (g2_ref[s] * dot(xnorm, ow, ((0,), (0,)))).astype(BF)
        gate_part += dot(normed, dgate, ((0,), (0,)))
        out_part += dot(xnorm, dout_ref[s])
        dgate_ref[s] = dgate
        proj = dot(w, normed, ((0,), (1,)))
        for n in range(2):
            val = proj[256 * n : 256 * n + 128]
            sig = jax.nn.sigmoid(proj[256 * n + 128 : 256 * n + 256])
            fac_ref[s, 256 * n : 256 * n + 128] = sig
            fac_ref[s, 256 * n + 128 : 256 * n + 256] = val * sig * (1.0 - sig)
    sum_ref[0:128] = gate_part.astype(BF)
    sum_ref[128:256] = out_part.astype(BF)


def pull_kernel(core_ref, own_ref, other_ref, a_ref, b_ref, msg_ref, dx, held):
    for n, ref in enumerate((own_ref, other_ref)):
        half = core_ref[0] if n == 0 else 1 - core_ref[0]
        for t in range(2):
            parts = [ref[t, :, q].astype(F32).reshape(128, 128) for q in range(4)]
            for g, part in enumerate(regroup(parts)):
                dx[half, pl.ds(128 * g, 128), pl.ds(128 * t, 128)] = part.astype(BF)
    da = dot(dx[0], b_ref[0]) + dot(dx[1], b_ref[1])
    for t in range(2):
        parts = [da[128 * g : 128 * g + 128, 128 * t : 128 * t + 128] for g in range(4)]
        for q, part in enumerate(regroup(parts)):
            held[t, :, :, q, 0:8] = part.reshape(8, 2, 8, 128)
    for half in range(2):
        db = dot(dx[half], a_ref[...], ((0,), (0,))).reshape(8, 4, 8, 256)
        for t in range(2):
            parts = [db[:, g, :, 128 * t : 128 * t + 128].reshape(64, 128) for g in range(4)]
            for q, part in enumerate(regroup(parts)):
                held[t, :, half, q, 8:16] = part.reshape(8, 8, 128)
    msg_ref[...] = held[...].astype(BF)


def weight_kernel(go_hbm, dab_ref, fac_ref, norm_ref, sum_hbm, dproj_ref, held, sums, sems):
    first = pltpu.make_async_copy(go_hbm, sum_hbm.at[pl.ds(512, 256)], sems.at[0])
    first.start()
    held[...] = dab_ref[...].astype(F32).reshape(2048, 128)
    total = jnp.zeros((512, 128), F32)
    for s in range(8):
        da = held[pl.ds(s, 128, stride=16), :]
        db = held[pl.ds(8 + s, 128, stride=16), :]
        fac = fac_ref[s]
        dproj = jnp.concatenate(
            [da * fac[0:128], da * fac[128:256], db * fac[256:384], db * fac[384:512]], axis=0
        ).astype(BF)
        dproj_ref[s] = dproj
        total += dot(dproj, norm_ref[s])
    sums[...] = total.astype(BF)
    last = pltpu.make_async_copy(sums, sum_hbm.at[pl.ds(0, 512)], sems.at[1])
    last.start()
    first.wait()
    last.wait()


def pair_kernel(dproj_ref, w_ref, dgate_ref, gw_ref, pair_ref, out_ref, token_ref):
    token_ref[...] = jnp.zeros((8, 128), F32)
    w = w_ref[...]
    gw = gw_ref[...]
    for s in range(8):
        zhat, zinv = layer_norm(pair_ref[:, s].astype(F32).reshape(128, 128))
        dnormed = dot(dproj_ref[s], w, ((0,), (1,))) + dot(dgate_ref[s], gw, ((1,), (1,)))
        grad = layer_norm_backward(dnormed, zhat, zinv)
        out_ref[:, s] = grad.reshape(4, 32, 128).astype(BF)


def sum_kernel(scale, parts_ref, out_ref):
    total = jnp.sum(parts_ref[...].astype(F32), axis=0, keepdims=True) * scale
    out_ref[...] = jnp.broadcast_to(total, out_ref.shape).astype(BF)


def collect_kernel(rows_ref, in_ref, gate_ref, out_ref):
    in_ref[...] = rows_ref[0:512].astype(F32).T
    gate_ref[...] = rows_ref[512:640].astype(F32)
    out_ref[...] = rows_ref[640:768].astype(F32)


def run(kernel, outs, *args, scratch=(), scalars=0, hbm=0, hbm_out=0, flops=0, after=(), grant=16):
    outs = [jax.ShapeDtypeStruct(shape, dtype) for shape, dtype in outs]
    vmem = pl.BlockSpec(memory_space=pltpu.VMEM)
    smem = pl.BlockSpec(memory_space=pltpu.SMEM)
    anywhere = pl.BlockSpec(memory_space=pltpu.HBM)
    skip = len(after)
    size = sum(v.size * v.dtype.itemsize for v in list(args) + outs)
    result = pl.pallas_call(
        lambda *refs: kernel(*refs[skip:]),
        out_shape=outs,
        in_specs=[anywhere] * (skip + hbm) + [smem] * scalars + [vmem] * (len(args) - scalars - hbm),
        out_specs=[anywhere] * hbm_out + [vmem] * (len(outs) - hbm_out),
        scratch_shapes=scratch,
        compiler_params=pltpu.CompilerParams(vmem_limit_bytes=grant * 1024 * 1024),
        cost_estimate=pl.CostEstimate(flops=flops, bytes_accessed=size, transcendentals=0),
    )(*after, *args)
    return result[0] if len(outs) == 1 else result


def exchange(values, axes):
    return lax.all_to_all(values, axes, 0, 0, tiled=True)


def per_device(pair, cotangent, in_weight, gate_weight, out_weight):
    core = jnp.reshape(lax.axis_index("core"), (1,)).astype(jnp.int32)
    pair = pair.reshape(4, 8, 32, 128)
    cotangent = cotangent.reshape(4, 8, 32, 128)

    msg, normed = run(
        project_kernel, [((128, 16, 128), BF), ((8, 128, 128), BF)], pair, in_weight, hbm=2, grant=56,
        scratch=[
            pltpu.VMEM((4, 8, 32, 128), BF), pltpu.VMEM((128, 512), BF),
            pltpu.VMEM((2048, 128), F32), pltpu.SemaphoreType.DMA((2,)),
        ],
        flops=134_000_000,
    )
    msg = exchange(msg, OWNERS).reshape(2, 8, 2, 4, 16, 128)
    g2, dout, dxnorm = run(
        side_kernel, [((8, 128, 128), F32), ((8, 128, 128), BF), ((1024, 128), F32)],
        normed, cotangent, gate_weight, out_weight, flops=67_000_000,
    )
    half = (2, 16, 4, 8, 128)
    a_own, b_own, give = run(
        pack_kernel, [((512, 256), BF), ((2, 256, 256), BF), (half, F32)],
        core, msg, scalars=1, flops=67_000_000,
    )
    got = lax.ppermute(give, "core", SWAP)
    keep = run(keep_kernel, [(half, F32)], core, a_own, b_own, scalars=1, flops=67_000_000)
    x = run(add_kernel, [(half, BF)], keep, got)
    x = exchange(x.reshape(128, 8, 128), OWNERS)
    dx, xhat = run(
        dx_kernel, [((128, 8, 128), BF), ((128, 8, 128), F32)], x, dxnorm.reshape(128, 8, 128), flops=1_000_000
    )
    dx = exchange(dx, OWNERS)
    dx = dx.reshape(2, 16, 4, 8, 128)
    other = lax.ppermute(dx, "core", SWAP)
    sums, dgate, factors = run(
        late_kernel, [((256, 128), BF), ((8, 128, 128), BF), ((8, 512, 128), F32)],
        xhat.reshape(1024, 128), normed, g2, dout, in_weight, out_weight, flops=268_000_000,
    )
    dab = run(
        pull_kernel, [((2, 8, 2, 4, 16, 128), BF)], core, dx, other, a_own, b_own, scalars=1, after=(sums,),
        scratch=[pltpu.VMEM((2, 512, 256), BF), pltpu.VMEM((2, 8, 2, 4, 16, 128), F32)], flops=268_000_000,
    )
    dab = exchange(dab.reshape(128, 16, 128), OWNERS)
    parts, dproj = run(
        weight_kernel, [((768, 128), BF), ((8, 512, 128), BF)],
        sums, dab, factors, normed, hbm=1, hbm_out=1,
        scratch=[
            pltpu.VMEM((2048, 128), F32), pltpu.VMEM((512, 128), BF), pltpu.SemaphoreType.DMA((2,)),
        ],
        flops=134_000_000,
    )
    parts = exchange(parts.reshape(32, 24, 128), PLANE)
    pair_grad, token = run(
        pair_kernel, [((4, 8, 32, 128), BF), ((8, 128), F32)], dproj, in_weight, dgate, gate_weight, pair,
        flops=134_000_000,
    )
    parts = run(functools.partial(sum_kernel, 1.0), [((8, 24, 128), BF)], parts, after=(token,))
    parts = exchange(parts, LINE)
    parts = run(functools.partial(sum_kernel, 1.0 / 512), [((32, 24, 128), BF)], parts)
    whole = exchange(parts, PLANE).reshape(768, 128)
    in_grad, gate_grad, out_grad = run(
        collect_kernel, [((128, 512), F32), ((128, 128), F32), ((128, 128), F32)], whole
    )
    return (pair_grad.reshape(32, 32, 128), in_grad, gate_grad, out_grad)


def solution(mesh):
    fine = Mesh(mesh.devices.reshape(4, 4, 2, 4, 2), ALL)
    tiles = P(ROW, CHI + ("core",), None)
    return jax.shard_map(
        per_device,
        mesh=fine,
        in_specs=(tiles, tiles, P(), P(), P()),
        out_specs=(tiles, P(), P(), P()),
        check_vma=False,
    )
```

```python
import functools

import jax
import jax.numpy as jnp
from jax import lax
from jax.experimental import pallas as pl
from jax.experimental.pallas import tpu as pltpu
from jax.sharding import Mesh, PartitionSpec as P

ROW = ("y", "zh")
CHI = ("zl", "x")
OWNERS = ("zl", "y", "zh", "x")
PLANE = ("core", "y", "x")
LINE = ("zh", "zl")
ALL = ("y", "zh", "zl", "x", "core")
SWAP = [(0, 1), (1, 0)]
BF = jnp.bfloat16
F32 = jnp.float32
EPS = 1e-05


def dot(left, right, contract=((1,), (0,))):
    return lax.dot_general(left, right, (contract, ((), ())), preferred_element_type=F32)


def layer_norm(values, axis=-1):
    center = values - jnp.mean(values, axis=axis, keepdims=True)
    scale = lax.rsqrt(jnp.mean(center * center, axis=axis, keepdims=True) + EPS)
    return center * scale, scale


def layer_norm_backward(grad, normal, scale, axis=-1):
    first = jnp.mean(grad, axis=axis, keepdims=True)
    second = jnp.mean(grad * normal, axis=axis, keepdims=True)
    return scale * (grad - first - normal * second)


def regroup(parts):
    lane = lax.broadcasted_iota(jnp.int32, parts[0].shape, 1)
    low = lane < 64
    even = (lane // 32) % 2 == 0
    p0, p1, p2, p3 = parts
    roll = lambda v, n: pltpu.roll(v, n, 1)
    p0, p2 = jnp.where(low, p0, roll(p2, 64)), jnp.where(low, roll(p0, 64), p2)
    p1, p3 = jnp.where(low, p1, roll(p3, 64)), jnp.where(low, roll(p1, 64), p3)
    p0, p1 = jnp.where(even, p0, roll(p1, 32)), jnp.where(even, roll(p0, 96), p1)
    p2, p3 = jnp.where(even, p2, roll(p3, 32)), jnp.where(even, roll(p2, 96), p3)
    return [p0, p1, p2, p3]


def project_kernel(pair_hbm, w_hbm, msg_ref, norm_ref, pair_ref, w_ref, held, sems):
    copies = [
        pltpu.make_async_copy(pair_hbm, pair_ref, sems.at[0]),
        pltpu.make_async_copy(w_hbm, w_ref, sems.at[1]),
    ]
    for copy in copies:
        copy.start()
    for copy in copies:
        copy.wait()
    w = w_ref[...]
    pair = jnp.concatenate([pair_ref[:, s].astype(F32).reshape(128, 128) for s in range(8)], axis=0)
    normed = layer_norm(pair)[0].astype(BF)
    norm_ref[...] = normed.reshape(8, 128, 128)
    for n in range(2):
        val = dot(w[:, 256 * n : 256 * n + 128], normed, ((0,), (1,)))
        sig = jax.nn.sigmoid(dot(w[:, 256 * n + 128 : 256 * n + 256], normed, ((0,), (1,))))
        val = val * sig
        for s in range(8):
            held[pl.ds(8 * n + s, 128, stride=16), :] = val[:, 128 * s : 128 * s + 128]
    msg_ref[...] = held[...].reshape(128, 16, 128).astype(BF)


def side_kernel(norm_ref, cot_ref, gw_ref, ow_ref, g2_ref, dout_ref, dxn_ref):
    gw = gw_ref[...]
    ow = ow_ref[...]
    for s in range(8):
        gate = jax.nn.sigmoid(dot(norm_ref[s], gw))
        upstream = cot_ref[:, s].astype(F32).reshape(128, 128)
        dout = upstream * gate
        g2_ref[s] = dout * (1.0 - gate)
        dout = dout.astype(BF)
        dout_ref[s] = dout
        dxn_ref[pl.ds(s, 128, stride=8), :] = dot(ow, dout, ((1,), (1,)))


def pack_a(msg_ref, a_ref):
    for t in range(2):
        parts = [msg_ref[t, :, :, q][:, :, 0:8].reshape(128, 128) for q in range(4)]
        for g, part in enumerate(regroup(parts)):
            a_ref[pl.ds(128 * g, 128), pl.ds(128 * t, 128)] = part


def pack_b(msg_ref, half, b_ref):
    for t in range(2):
        parts = [msg_ref[t, :, half, q][:, 8:16].reshape(64, 128) for q in range(4)]
        parts = [part.reshape(8, 8, 128) for part in regroup(parts)]
        b_ref[:, pl.ds(128 * t, 128)] = jnp.stack(parts, axis=1).reshape(256, 128)


def pack_kernel(msg_ref, a_ref, b_ref):
    pack_a(msg_ref, a_ref)
    for half in range(2):
        pack_b(msg_ref, half, b_ref.at[half])


def x_kernel(core_ref, a_ref, b_ref, other_ref, msg_ref, oa_ref, ob_ref):
    core = core_ref[0]
    pack_a(other_ref, oa_ref)
    pack_b(other_ref, core, ob_ref)
    x = dot(a_ref[...], b_ref[core], ((1,), (1,))) + dot(oa_ref[...], ob_ref[...], ((1,), (1,)))
    for t in range(2):
        parts = [x[128 * g : 128 * g + 128, 128 * t : 128 * t + 128] for g in range(4)]
        for q, part in enumerate(regroup(parts)):
            msg_ref[t, :, q] = part.reshape(16, 8, 128).astype(BF)


def dx_kernel(x_ref, dxn_ref, msg_ref, xhat_ref):
    xhat, xinv = layer_norm(x_ref[...].astype(F32), 0)
    xhat_ref[...] = xhat
    msg_ref[...] = layer_norm_backward(dxn_ref[...], xhat, xinv, 0).astype(BF)


def late_kernel(xhat_ref, norm_ref, g2_ref, dout_ref, w_ref, ow_ref, sum_ref, dgate_ref, fac_ref):
    w = w_ref[...]
    ow = ow_ref[...]
    gate_part = jnp.zeros((128, 128), F32)
    out_part = jnp.zeros((128, 128), F32)
    for s in range(8):
        normed = norm_ref[s]
        xnorm = xhat_ref[pl.ds(s, 128, stride=8), :].astype(BF)
        dgate = (g2_ref[s] * dot(xnorm, ow, ((0,), (0,)))).astype(BF)
        gate_part += dot(normed, dgate, ((0,), (0,)))
        out_part += dot(xnorm, dout_ref[s])
        dgate_ref[s] = dgate
        proj = dot(w, normed, ((0,), (1,)))
        for n in range(2):
            val = proj[256 * n : 256 * n + 128]
            sig = jax.nn.sigmoid(proj[256 * n + 128 : 256 * n + 256])
            fac_ref[s, 256 * n : 256 * n + 128] = sig
            fac_ref[s, 256 * n + 128 : 256 * n + 256] = val * sig * (1.0 - sig)
    sum_ref[0:128] = gate_part.astype(BF)
    sum_ref[128:256] = out_part.astype(BF)


def pull_kernel(core_ref, own_ref, other_ref, a_ref, b_ref, msg_ref, dx, held):
    for n, ref in enumerate((own_ref, other_ref)):
        half = core_ref[0] if n == 0 else 1 - core_ref[0]
        for t in range(2):
            parts = [ref[t, :, q].reshape(128, 128) for q in range(4)]
            for g, part in enumerate(regroup(parts)):
                dx[half, pl.ds(128 * g, 128), pl.ds(128 * t, 128)] = part
    da = dot(dx[0], b_ref[0]) + dot(dx[1], b_ref[1])
    for t in range(2):
        parts = [da[128 * g : 128 * g + 128, 128 * t : 128 * t + 128] for g in range(4)]
        for q, part in enumerate(regroup(parts)):
            held[t, :, :, q, 0:8] = part.reshape(8, 2, 8, 128)
    for half in range(2):
        db = dot(dx[half], a_ref[...], ((0,), (0,))).reshape(8, 4, 8, 256)
        for t in range(2):
            parts = [db[:, g, :, 128 * t : 128 * t + 128].reshape(64, 128) for g in range(4)]
            for q, part in enumerate(regroup(parts)):
                held[t, :, half, q, 8:16] = part.reshape(8, 8, 128)
    msg_ref[...] = held[...].astype(BF)


def weight_kernel(go_hbm, dab_ref, fac_ref, norm_ref, sum_hbm, dproj_ref, held, sums, sems):
    first = pltpu.make_async_copy(go_hbm, sum_hbm.at[pl.ds(512, 256)], sems.at[0])
    first.start()
    held[...] = dab_ref[...].astype(F32).reshape(2048, 128)
    total = jnp.zeros((512, 128), F32)
    for s in range(8):
        da = held[pl.ds(s, 128, stride=16), :]
        db = held[pl.ds(8 + s, 128, stride=16), :]
        fac = fac_ref[s]
        dproj = jnp.concatenate(
            [da * fac[0:128], da * fac[128:256], db * fac[256:384], db * fac[384:512]], axis=0
        ).astype(BF)
        dproj_ref[s] = dproj
        total += dot(dproj, norm_ref[s])
    sums[...] = total.astype(BF)
    last = pltpu.make_async_copy(sums, sum_hbm.at[pl.ds(0, 512)], sems.at[1])
    last.start()
    first.wait()
    last.wait()


def pair_kernel(dproj_ref, w_ref, dgate_ref, gw_ref, pair_ref, out_ref, token_ref):
    token_ref[...] = jnp.zeros((8, 128), F32)
    w = w_ref[...]
    gw = gw_ref[...]
    for s in range(8):
        zhat, zinv = layer_norm(pair_ref[:, s].astype(F32).reshape(128, 128))
        dnormed = dot(dproj_ref[s], w, ((0,), (1,))) + dot(dgate_ref[s], gw, ((1,), (1,)))
        grad = layer_norm_backward(dnormed, zhat, zinv)
        out_ref[:, s] = grad.reshape(4, 32, 128).astype(BF)


def sum_kernel(scale, parts_ref, out_ref):
    total = jnp.sum(parts_ref[...].astype(F32), axis=0, keepdims=True) * scale
    out_ref[...] = jnp.broadcast_to(total, out_ref.shape).astype(BF)


def collect_kernel(rows_ref, in_ref, gate_ref, out_ref):
    in_ref[...] = rows_ref[0:512].astype(F32).T
    gate_ref[...] = rows_ref[512:640].astype(F32)
    out_ref[...] = rows_ref[640:768].astype(F32)


def run(kernel, outs, *args, scratch=(), scalars=0, hbm=0, hbm_out=0, flops=0, after=(), grant=16):
    outs = [jax.ShapeDtypeStruct(shape, dtype) for shape, dtype in outs]
    vmem = pl.BlockSpec(memory_space=pltpu.VMEM)
    smem = pl.BlockSpec(memory_space=pltpu.SMEM)
    anywhere = pl.BlockSpec(memory_space=pltpu.HBM)
    skip = len(after)
    size = sum(v.size * v.dtype.itemsize for v in list(args) + outs)
    result = pl.pallas_call(
        lambda *refs: kernel(*refs[skip:]),
        out_shape=outs,
        in_specs=[anywhere] * (skip + hbm) + [smem] * scalars + [vmem] * (len(args) - scalars - hbm),
        out_specs=[anywhere] * hbm_out + [vmem] * (len(outs) - hbm_out),
        scratch_shapes=scratch,
        compiler_params=pltpu.CompilerParams(vmem_limit_bytes=grant * 1024 * 1024),
        cost_estimate=pl.CostEstimate(flops=flops, bytes_accessed=size, transcendentals=0),
    )(*after, *args)
    return result[0] if len(outs) == 1 else result


def exchange(values, axes):
    return lax.all_to_all(values, axes, 0, 0, tiled=True)


def per_device(pair, cotangent, in_weight, gate_weight, out_weight):
    core = jnp.reshape(lax.axis_index("core"), (1,)).astype(jnp.int32)
    pair = pair.reshape(4, 8, 32, 128)
    cotangent = cotangent.reshape(4, 8, 32, 128)

    msg, normed = run(
        project_kernel, [((128, 16, 128), BF), ((8, 128, 128), BF)], pair, in_weight, hbm=2, grant=56,
        scratch=[
            pltpu.VMEM((4, 8, 32, 128), BF), pltpu.VMEM((128, 512), BF),
            pltpu.VMEM((2048, 128), F32), pltpu.SemaphoreType.DMA((2,)),
        ],
        flops=134_000_000,
    )
    msg = exchange(msg, OWNERS).reshape(2, 8, 2, 4, 16, 128)
    g2, dout, dxnorm = run(
        side_kernel, [((8, 128, 128), F32), ((8, 128, 128), BF), ((1024, 128), F32)],
        normed, cotangent, gate_weight, out_weight, flops=67_000_000,
    )
    other = lax.ppermute(msg, "core", SWAP)
    a_own, b_own = run(pack_kernel, [((512, 256), BF), ((2, 256, 256), BF)], msg, flops=1_000_000)
    x = run(
        x_kernel, [((2, 16, 4, 8, 128), BF)], core, a_own, b_own, other, scalars=1, flops=134_000_000,
        scratch=[pltpu.VMEM((512, 256), BF), pltpu.VMEM((256, 256), BF)],
    )
    x = exchange(x.reshape(128, 8, 128), OWNERS)
    dx, xhat = run(
        dx_kernel, [((128, 8, 128), BF), ((128, 8, 128), F32)], x, dxnorm.reshape(128, 8, 128), flops=1_000_000
    )
    dx = exchange(dx, OWNERS)
    dx = dx.reshape(2, 16, 4, 8, 128)
    other = lax.ppermute(dx, "core", SWAP)
    sums, dgate, factors = run(
        late_kernel, [((256, 128), BF), ((8, 128, 128), BF), ((8, 512, 128), F32)],
        xhat.reshape(1024, 128), normed, g2, dout, in_weight, out_weight, flops=268_000_000,
    )
    dab = run(
        pull_kernel, [((2, 8, 2, 4, 16, 128), BF)], core, dx, other, a_own, b_own, scalars=1, after=(sums,),
        scratch=[pltpu.VMEM((2, 512, 256), BF), pltpu.VMEM((2, 8, 2, 4, 16, 128), F32)], flops=268_000_000,
    )
    dab = exchange(dab.reshape(128, 16, 128), OWNERS)
    parts, dproj = run(
        weight_kernel, [((768, 128), BF), ((8, 512, 128), BF)],
        sums, dab, factors, normed, hbm=1, hbm_out=1,
        scratch=[
            pltpu.VMEM((2048, 128), F32), pltpu.VMEM((512, 128), BF), pltpu.SemaphoreType.DMA((2,)),
        ],
        flops=134_000_000,
    )
    parts = exchange(parts.reshape(32, 24, 128), PLANE)
    pair_grad, token = run(
        pair_kernel, [((4, 8, 32, 128), BF), ((8, 128), F32)], dproj, in_weight, dgate, gate_weight, pair,
        flops=134_000_000,
    )
    parts = run(functools.partial(sum_kernel, 1.0), [((8, 24, 128), BF)], parts, after=(token,))
    parts = exchange(parts, LINE)
    parts = run(functools.partial(sum_kernel, 1.0 / 512), [((32, 24, 128), BF)], parts)
    whole = exchange(parts, PLANE).reshape(768, 128)
    in_grad, gate_grad, out_grad = run(
        collect_kernel, [((128, 512), F32), ((128, 128), F32), ((128, 128), F32)], whole
    )
    return (pair_grad.reshape(32, 32, 128), in_grad, gate_grad, out_grad)


def solution(mesh):
    fine = Mesh(mesh.devices.reshape(4, 4, 2, 4, 2), ALL)
    tiles = P(ROW, CHI + ("core",), None)
    return jax.shard_map(
        per_device,
        mesh=fine,
        in_specs=(tiles, tiles, P(), P(), P()),
        out_specs=(tiles, P(), P(), P()),
        check_vma=False,
    )
```

```python
import functools

import jax
import jax.numpy as jnp
from jax import lax
from jax.experimental import pallas as pl
from jax.experimental.pallas import tpu as pltpu
from jax.sharding import Mesh, PartitionSpec as P

ROW = ("y", "zh")
CHI = ("zl", "x")
OWNERS = ("zl", "y", "zh", "x")
PLANE = ("core", "y", "x")
LINE = ("zh", "zl")
ALL = ("y", "zh", "zl", "x", "core")
SWAP = [(0, 1), (1, 0)]
BF = jnp.bfloat16
F32 = jnp.float32
EPS = 1e-05


def dot(left, right, contract=((1,), (0,))):
    return lax.dot_general(left, right, (contract, ((), ())), preferred_element_type=F32)


def layer_norm(values, axis=-1):
    center = values - jnp.mean(values, axis=axis, keepdims=True)
    scale = lax.rsqrt(jnp.mean(center * center, axis=axis, keepdims=True) + EPS)
    return center * scale, scale


def layer_norm_backward(grad, normal, scale, axis=-1):
    first = jnp.mean(grad, axis=axis, keepdims=True)
    second = jnp.mean(grad * normal, axis=axis, keepdims=True)
    return scale * (grad - first - normal * second)


def regroup(parts):
    lane = lax.broadcasted_iota(jnp.int32, parts[0].shape, 1)
    low = lane < 64
    even = (lane // 32) % 2 == 0
    p0, p1, p2, p3 = parts
    roll = lambda v, n: pltpu.roll(v, n, 1)
    p0, p2 = jnp.where(low, p0, roll(p2, 64)), jnp.where(low, roll(p0, 64), p2)
    p1, p3 = jnp.where(low, p1, roll(p3, 64)), jnp.where(low, roll(p1, 64), p3)
    p0, p1 = jnp.where(even, p0, roll(p1, 32)), jnp.where(even, roll(p0, 96), p1)
    p2, p3 = jnp.where(even, p2, roll(p3, 32)), jnp.where(even, roll(p2, 96), p3)
    return [p0, p1, p2, p3]


def project_kernel(pair_hbm, w_hbm, msg_ref, norm_ref, pair_ref, w_ref, held, sems):
    copies = [
        pltpu.make_async_copy(pair_hbm, pair_ref, sems.at[0]),
        pltpu.make_async_copy(w_hbm, w_ref, sems.at[1]),
    ]
    for copy in copies:
        copy.start()
    for copy in copies:
        copy.wait()
    w = w_ref[...]
    pair = jnp.concatenate([pair_ref[:, s].astype(F32).reshape(128, 128) for s in range(8)], axis=0)
    normed = layer_norm(pair)[0].astype(BF)
    norm_ref[...] = normed.reshape(8, 128, 128)
    for n in range(2):
        val = dot(w[:, 256 * n : 256 * n + 128], normed, ((0,), (1,)))
        sig = jax.nn.sigmoid(dot(w[:, 256 * n + 128 : 256 * n + 256], normed, ((0,), (1,))))
        val = val * sig
        for s in range(8):
            held[pl.ds(8 * n + s, 128, stride=16), :] = val[:, 128 * s : 128 * s + 128]
    msg_ref[...] = held[...].reshape(128, 16, 128).astype(BF)


def side_kernel(norm_ref, cot_ref, gw_ref, ow_ref, g2_ref, dout_ref, dxn_ref):
    gw = gw_ref[...]
    ow = ow_ref[...]
    for s in range(8):
        gate = jax.nn.sigmoid(dot(norm_ref[s], gw))
        upstream = cot_ref[:, s].astype(F32).reshape(128, 128)
        dout = upstream * gate
        g2_ref[s] = dout * (1.0 - gate)
        dout = dout.astype(BF)
        dout_ref[s] = dout
        dxn_ref[pl.ds(s, 128, stride=8), :] = dot(ow, dout, ((1,), (1,)))


def pack_a(msg_ref, a_ref):
    for t in range(2):
        parts = [msg_ref[t, :, :, q].astype(F32)[:, :, 0:8].reshape(128, 128) for q in range(4)]
        for g, part in enumerate(regroup(parts)):
            a_ref[pl.ds(128 * g, 128), pl.ds(128 * t, 128)] = part.astype(BF)


def pack_b(msg_ref, half, b_ref):
    for t in range(2):
        parts = [msg_ref[t, :, half, q].astype(F32)[:, 8:16].reshape(64, 128) for q in range(4)]
        parts = [part.reshape(8, 8, 128) for part in regroup(parts)]
        b_ref[:, pl.ds(128 * t, 128)] = jnp.stack(parts, axis=1).reshape(256, 128).astype(BF)


def pack_kernel(msg_ref, a_ref, b_ref):
    pack_a(msg_ref, a_ref)
    for half in range(2):
        pack_b(msg_ref, half, b_ref.at[half])


def x_kernel(core_ref, a_ref, b_ref, other_ref, msg_ref, oa_ref, ob_ref):
    core = core_ref[0]
    pack_a(other_ref, oa_ref)
    pack_b(other_ref, core, ob_ref)
    x = dot(a_ref[...], b_ref[core], ((1,), (1,))) + dot(oa_ref[...], ob_ref[...], ((1,), (1,)))
    for t in range(2):
        parts = [x[128 * g : 128 * g + 128, 128 * t : 128 * t + 128] for g in range(4)]
        for q, part in enumerate(regroup(parts)):
            msg_ref[t, :, q] = part.reshape(16, 8, 128).astype(BF)


def dx_kernel(x_ref, dxn_ref, msg_ref, xhat_ref):
    xhat, xinv = layer_norm(x_ref[...].astype(F32), 0)
    xhat_ref[...] = xhat
    msg_ref[...] = layer_norm_backward(dxn_ref[...], xhat, xinv, 0).astype(BF)


def late_kernel(xhat_ref, norm_ref, g2_ref, dout_ref, w_ref, ow_ref, sum_ref, dgate_ref, fac_ref):
    w = w_ref[...]
    ow = ow_ref[...]
    gate_part = jnp.zeros((128, 128), F32)
    out_part = jnp.zeros((128, 128), F32)
    for s in range(8):
        normed = norm_ref[s]
        xnorm = xhat_ref[pl.ds(s, 128, stride=8), :].astype(BF)
        dgate = (g2_ref[s] * dot(xnorm, ow, ((0,), (0,)))).astype(BF)
        gate_part += dot(normed, dgate, ((0,), (0,)))
        out_part += dot(xnorm, dout_ref[s])
        dgate_ref[s] = dgate
        proj = dot(w, normed, ((0,), (1,)))
        for n in range(2):
            val = proj[256 * n : 256 * n + 128]
            sig = jax.nn.sigmoid(proj[256 * n + 128 : 256 * n + 256])
            fac_ref[s, 256 * n : 256 * n + 128] = sig
            fac_ref[s, 256 * n + 128 : 256 * n + 256] = val * sig * (1.0 - sig)
    sum_ref[0:128] = gate_part.astype(BF)
    sum_ref[128:256] = out_part.astype(BF)


def pull_kernel(core_ref, own_ref, other_ref, a_ref, b_ref, msg_ref, dx, held):
    for n, ref in enumerate((own_ref, other_ref)):
        half = core_ref[0] if n == 0 else 1 - core_ref[0]
        for t in range(2):
            parts = [ref[t, :, q].astype(F32).reshape(128, 128) for q in range(4)]
            for g, part in enumerate(regroup(parts)):
                dx[half, pl.ds(128 * g, 128), pl.ds(128 * t, 128)] = part.astype(BF)
    da = dot(dx[0], b_ref[0]) + dot(dx[1], b_ref[1])
    for t in range(2):
        parts = [da[128 * g : 128 * g + 128, 128 * t : 128 * t + 128] for g in range(4)]
        for q, part in enumerate(regroup(parts)):
            held[t, :, :, q, 0:8] = part.reshape(8, 2, 8, 128)
    for half in range(2):
        db = dot(dx[half], a_ref[...], ((0,), (0,))).reshape(8, 4, 8, 256)
        for t in range(2):
            parts = [db[:, g, :, 128 * t : 128 * t + 128].reshape(64, 128) for g in range(4)]
            for q, part in enumerate(regroup(parts)):
                held[t, :, half, q, 8:16] = part.reshape(8, 8, 128)
    msg_ref[...] = held[...].astype(BF)


def weight_kernel(go_hbm, dab_ref, fac_ref, norm_ref, sum_hbm, dproj_ref, held, sums, sems):
    first = pltpu.make_async_copy(go_hbm, sum_hbm.at[pl.ds(512, 256)], sems.at[0])
    first.start()
    held[...] = dab_ref[...].astype(F32).reshape(2048, 128)
    total = jnp.zeros((512, 128), F32)
    for s in range(8):
        da = held[pl.ds(s, 128, stride=16), :]
        db = held[pl.ds(8 + s, 128, stride=16), :]
        fac = fac_ref[s]
        dproj = jnp.concatenate(
            [da * fac[0:128], da * fac[128:256], db * fac[256:384], db * fac[384:512]], axis=0
        ).astype(BF)
        dproj_ref[s] = dproj
        total += dot(dproj, norm_ref[s])
    sums[...] = total.astype(BF)
    last = pltpu.make_async_copy(sums, sum_hbm.at[pl.ds(0, 512)], sems.at[1])
    last.start()
    first.wait()
    last.wait()


def pair_kernel(dproj_ref, w_ref, dgate_ref, gw_ref, pair_ref, out_ref, token_ref):
    token_ref[...] = jnp.zeros((8, 128), F32)
    w = w_ref[...]
    gw = gw_ref[...]
    for s in range(8):
        zhat, zinv = layer_norm(pair_ref[:, s].astype(F32).reshape(128, 128))
        dnormed = dot(dproj_ref[s], w, ((0,), (1,))) + dot(dgate_ref[s], gw, ((1,), (1,)))
        grad = layer_norm_backward(dnormed, zhat, zinv)
        out_ref[:, s] = grad.reshape(4, 32, 128).astype(BF)


def sum_kernel(scale, parts_ref, out_ref):
    total = jnp.sum(parts_ref[...].astype(F32), axis=0, keepdims=True) * scale
    out_ref[...] = jnp.broadcast_to(total, out_ref.shape).astype(BF)


def collect_kernel(rows_ref, in_ref, gate_ref, out_ref):
    in_ref[...] = rows_ref[0:512].astype(F32).T
    gate_ref[...] = rows_ref[512:640].astype(F32)
    out_ref[...] = rows_ref[640:768].astype(F32)


def run(kernel, outs, *args, scratch=(), scalars=0, hbm=0, hbm_out=0, flops=0, after=(), grant=16):
    outs = [jax.ShapeDtypeStruct(shape, dtype) for shape, dtype in outs]
    vmem = pl.BlockSpec(memory_space=pltpu.VMEM)
    smem = pl.BlockSpec(memory_space=pltpu.SMEM)
    anywhere = pl.BlockSpec(memory_space=pltpu.HBM)
    skip = len(after)
    size = sum(v.size * v.dtype.itemsize for v in list(args) + outs)
    result = pl.pallas_call(
        lambda *refs: kernel(*refs[skip:]),
        out_shape=outs,
        in_specs=[anywhere] * (skip + hbm) + [smem] * scalars + [vmem] * (len(args) - scalars - hbm),
        out_specs=[anywhere] * hbm_out + [vmem] * (len(outs) - hbm_out),
        scratch_shapes=scratch,
        compiler_params=pltpu.CompilerParams(vmem_limit_bytes=grant * 1024 * 1024),
        cost_estimate=pl.CostEstimate(flops=flops, bytes_accessed=size, transcendentals=0),
    )(*after, *args)
    return result[0] if len(outs) == 1 else result


def exchange(values, axes):
    return lax.all_to_all(values, axes, 0, 0, tiled=True)


def per_device(pair, cotangent, in_weight, gate_weight, out_weight):
    core = jnp.reshape(lax.axis_index("core"), (1,)).astype(jnp.int32)
    pair = pair.reshape(4, 8, 32, 128)
    cotangent = cotangent.reshape(4, 8, 32, 128)

    msg, normed = run(
        project_kernel, [((128, 16, 128), BF), ((8, 128, 128), BF)], pair, in_weight, hbm=2, grant=56,
        scratch=[
            pltpu.VMEM((4, 8, 32, 128), BF), pltpu.VMEM((128, 512), BF),
            pltpu.VMEM((2048, 128), F32), pltpu.SemaphoreType.DMA((2,)),
        ],
        flops=134_000_000,
    )
    msg = exchange(msg, OWNERS).reshape(2, 8, 2, 4, 16, 128)
    g2, dout, dxnorm = run(
        side_kernel, [((8, 128, 128), F32), ((8, 128, 128), BF), ((1024, 128), F32)],
        normed, cotangent, gate_weight, out_weight, flops=67_000_000,
    )
    other = lax.ppermute(msg, "core", SWAP)
    a_own, b_own = run(pack_kernel, [((512, 256), BF), ((2, 256, 256), BF)], msg, flops=1_000_000)
    x = run(
        x_kernel, [((2, 16, 4, 8, 128), BF)], core, a_own, b_own, other, scalars=1, flops=134_000_000,
        scratch=[pltpu.VMEM((512, 256), BF), pltpu.VMEM((256, 256), BF)],
    )
    x = exchange(x.reshape(128, 8, 128), OWNERS)
    dx, xhat = run(
        dx_kernel, [((128, 8, 128), BF), ((128, 8, 128), F32)], x, dxnorm.reshape(128, 8, 128), flops=1_000_000
    )
    dx = exchange(dx, OWNERS)
    dx = dx.reshape(2, 16, 4, 8, 128)
    other = lax.ppermute(dx, "core", SWAP)
    sums, dgate, factors = run(
        late_kernel, [((256, 128), BF), ((8, 128, 128), BF), ((8, 512, 128), F32)],
        xhat.reshape(1024, 128), normed, g2, dout, in_weight, out_weight, flops=268_000_000,
    )
    dab = run(
        pull_kernel, [((2, 8, 2, 4, 16, 128), BF)], core, dx, other, a_own, b_own, scalars=1, after=(sums,),
        scratch=[pltpu.VMEM((2, 512, 256), BF), pltpu.VMEM((2, 8, 2, 4, 16, 128), F32)], flops=268_000_000,
    )
    dab = exchange(dab.reshape(128, 16, 128), OWNERS)
    parts, dproj = run(
        weight_kernel, [((768, 128), BF), ((8, 512, 128), BF)],
        sums, dab, factors, normed, hbm=1, hbm_out=1,
        scratch=[
            pltpu.VMEM((2048, 128), F32), pltpu.VMEM((512, 128), BF), pltpu.SemaphoreType.DMA((2,)),
        ],
        flops=134_000_000,
    )
    parts = exchange(parts.reshape(32, 24, 128), PLANE)
    pair_grad, token = run(
        pair_kernel, [((4, 8, 32, 128), BF), ((8, 128), F32)], dproj, in_weight, dgate, gate_weight, pair,
        flops=134_000_000,
    )
    parts = run(functools.partial(sum_kernel, 1.0), [((8, 24, 128), BF)], parts, after=(token,))
    parts = exchange(parts, LINE)
    parts = run(functools.partial(sum_kernel, 1.0 / 512), [((32, 24, 128), BF)], parts)
    whole = exchange(parts, PLANE).reshape(768, 128)
    in_grad, gate_grad, out_grad = run(
        collect_kernel, [((128, 512), F32), ((128, 128), F32), ((128, 128), F32)], whole
    )
    return (pair_grad.reshape(32, 32, 128), in_grad, gate_grad, out_grad)


def solution(mesh):
    fine = Mesh(mesh.devices.reshape(4, 4, 2, 4, 2), ALL)
    tiles = P(ROW, CHI + ("core",), None)
    return jax.shard_map(
        per_device,
        mesh=fine,
        in_specs=(tiles, tiles, P(), P(), P()),
        out_specs=(tiles, P(), P(), P()),
        check_vma=False,
    )
```

```python
import functools

import jax
import jax.numpy as jnp
from jax import lax
from jax.experimental import pallas as pl
from jax.experimental.pallas import tpu as pltpu
from jax.sharding import Mesh, PartitionSpec as P

ROW = ("y", "zh")
CHI = ("zl", "x")
OWNERS = ("zl", "y", "zh", "x")
PLANE = ("core", "y", "x")
LINE = ("zh", "zl")
ALL = ("y", "zh", "zl", "x", "core")
SWAP = [(0, 1), (1, 0)]
BF = jnp.bfloat16
F32 = jnp.float32
EPS = 1e-05


def dot(left, right, contract=((1,), (0,))):
    return lax.dot_general(left, right, (contract, ((), ())), preferred_element_type=F32)


def layer_norm(values, axis=-1):
    center = values - jnp.mean(values, axis=axis, keepdims=True)
    scale = lax.rsqrt(jnp.mean(center * center, axis=axis, keepdims=True) + EPS)
    return center * scale, scale


def layer_norm_backward(grad, normal, scale, axis=-1):
    first = jnp.mean(grad, axis=axis, keepdims=True)
    second = jnp.mean(grad * normal, axis=axis, keepdims=True)
    return scale * (grad - first - normal * second)


def regroup(parts):
    lane = lax.broadcasted_iota(jnp.int32, parts[0].shape, 1)
    low = lane < 64
    even = (lane // 32) % 2 == 0
    p0, p1, p2, p3 = parts
    roll = lambda v, n: pltpu.roll(v, n, 1)
    p0, p2 = jnp.where(low, p0, roll(p2, 64)), jnp.where(low, roll(p0, 64), p2)
    p1, p3 = jnp.where(low, p1, roll(p3, 64)), jnp.where(low, roll(p1, 64), p3)
    p0, p1 = jnp.where(even, p0, roll(p1, 32)), jnp.where(even, roll(p0, 96), p1)
    p2, p3 = jnp.where(even, p2, roll(p3, 32)), jnp.where(even, roll(p2, 96), p3)
    return [p0, p1, p2, p3]


def project_kernel(pair_hbm, w_hbm, msg_ref, norm_ref, pair_ref, w_ref, held, sems):
    copies = [
        pltpu.make_async_copy(pair_hbm, pair_ref, sems.at[0]),
        pltpu.make_async_copy(w_hbm, w_ref, sems.at[1]),
    ]
    for copy in copies:
        copy.start()
    for copy in copies:
        copy.wait()
    w = w_ref[...]
    pair = jnp.concatenate([pair_ref[:, s].astype(F32).reshape(128, 128) for s in range(8)], axis=0)
    normed = layer_norm(pair)[0].astype(BF)
    norm_ref[...] = normed.reshape(8, 128, 128)
    for n in range(2):
        val = dot(w[:, 256 * n : 256 * n + 128], normed, ((0,), (1,)))
        sig = jax.nn.sigmoid(dot(w[:, 256 * n + 128 : 256 * n + 256], normed, ((0,), (1,))))
        val = val * sig
        for s in range(8):
            held[pl.ds(8 * n + s, 128, stride=16), :] = val[:, 128 * s : 128 * s + 128]
    msg_ref[...] = held[...].reshape(128, 16, 128).astype(BF)


def side_kernel(norm_ref, cot_ref, gw_ref, ow_ref, g2_ref, dout_ref, dxn_ref):
    gw = gw_ref[...]
    ow = ow_ref[...]
    for s in range(8):
        gate = jax.nn.sigmoid(dot(norm_ref[s], gw))
        upstream = cot_ref[:, s].astype(F32).reshape(128, 128)
        dout = upstream * gate
        g2_ref[s] = (dout * (1.0 - gate)).T
        dout = dout.astype(BF)
        dout_ref[s] = dout
        dxn_ref[pl.ds(s, 128, stride=8), :] = dot(ow, dout, ((1,), (1,)))


def pack_a(msg_ref, a_ref):
    for t in range(2):
        parts = [msg_ref[t, :, :, q].astype(F32)[:, :, 0:8].reshape(128, 128) for q in range(4)]
        for g, part in enumerate(regroup(parts)):
            a_ref[pl.ds(128 * g, 128), pl.ds(128 * t, 128)] = part.astype(BF)


def pack_b(msg_ref, half, b_ref):
    for t in range(2):
        parts = [msg_ref[t, :, half, q].astype(F32)[:, 8:16].reshape(64, 128) for q in range(4)]
        parts = [part.reshape(8, 8, 128) for part in regroup(parts)]
        b_ref[:, pl.ds(128 * t, 128)] = jnp.stack(parts, axis=1).reshape(256, 128).astype(BF)


def pack_kernel(core_ref, msg_ref, a_ref, b_ref, send_ref):
    pack_a(msg_ref, a_ref)
    for half in range(2):
        pack_b(msg_ref, half, b_ref.at[half])
    send_ref[0:512] = a_ref[...]
    send_ref[512:768] = b_ref[1 - core_ref[0]]


def keep_kernel(core_ref, a_ref, b_ref, keep_ref):
    keep_ref[...] = dot(a_ref[...], b_ref[core_ref[0]], ((1,), (1,)))


def x_kernel(keep_ref, got_ref, msg_ref):
    x = keep_ref[...] + dot(got_ref[0:512], got_ref[512:768], ((1,), (1,)))
    for t in range(2):
        parts = [x[128 * g : 128 * g + 128, 128 * t : 128 * t + 128] for g in range(4)]
        for q, part in enumerate(regroup(parts)):
            msg_ref[t, :, q] = part.reshape(16, 8, 128).astype(BF)


def dx_kernel(x_ref, dxn_ref, msg_ref, xhat_ref):
    xhat, xinv = layer_norm(x_ref[...].astype(F32), 0)
    xhat_ref[...] = xhat
    msg_ref[...] = layer_norm_backward(dxn_ref[...], xhat, xinv, 0).astype(BF)


def late_kernel(xhat_ref, norm_ref, g2_ref, dout_ref, w_ref, ow_ref, sum_ref, dgate_ref, fac_ref):
    w = w_ref[...]
    ow = ow_ref[...].T
    gate_part = jnp.zeros((128, 128), F32)
    out_part = jnp.zeros((128, 128), F32)
    for s in range(8):
        normed = norm_ref[s]
        xnorm = xhat_ref[pl.ds(s, 128, stride=8), :].astype(BF)
        dgate = (g2_ref[s] * dot(ow, xnorm)).astype(BF)
        gate_part += dot(dgate, normed)
        out_part += dot(xnorm, dout_ref[s])
        dgate_ref[s] = dgate
        proj = dot(w, normed, ((0,), (1,)))
        for n in range(2):
            val = proj[256 * n : 256 * n + 128]
            sig = jax.nn.sigmoid(proj[256 * n + 128 : 256 * n + 256])
            fac_ref[s, 256 * n : 256 * n + 128] = sig
            fac_ref[s, 256 * n + 128 : 256 * n + 256] = val * sig * (1.0 - sig)
    sum_ref[0:128] = gate_part.T.astype(BF)
    sum_ref[128:256] = out_part.astype(BF)


def pull_kernel(core_ref, own_ref, other_ref, a_ref, b_ref, msg_ref, dx, held):
    for n, ref in enumerate((own_ref, other_ref)):
        half = core_ref[0] if n == 0 else 1 - core_ref[0]
        for t in range(2):
            parts = [ref[t, :, q].astype(F32).reshape(128, 128) for q in range(4)]
            for g, part in enumerate(regroup(parts)):
                dx[half, pl.ds(128 * g, 128), pl.ds(128 * t, 128)] = part.astype(BF)
    da = dot(dx[0], b_ref[0]) + dot(dx[1], b_ref[1])
    for t in range(2):
        parts = [da[128 * g : 128 * g + 128, 128 * t : 128 * t + 128] for g in range(4)]
        for q, part in enumerate(regroup(parts)):
            held[t, :, :, q, 0:8] = part.reshape(8, 2, 8, 128)
    for half in range(2):
        db = dot(dx[half], a_ref[...], ((0,), (0,))).reshape(8, 4, 8, 256)
        for t in range(2):
            parts = [db[:, g, :, 128 * t : 128 * t + 128].reshape(64, 128) for g in range(4)]
            for q, part in enumerate(regroup(parts)):
                held[t, :, half, q, 8:16] = part.reshape(8, 8, 128)
    msg_ref[...] = held[...].astype(BF)


def weight_kernel(go_hbm, dab_ref, fac_ref, norm_ref, sum_hbm, dproj_ref, held, sums, sems):
    first = pltpu.make_async_copy(go_hbm, sum_hbm.at[pl.ds(512, 256)], sems.at[0])
    first.start()
    held[...] = dab_ref[...].astype(F32).reshape(2048, 128)
    total = jnp.zeros((512, 128), F32)
    for s in range(8):
        da = held[pl.ds(s, 128, stride=16), :]
        db = held[pl.ds(8 + s, 128, stride=16), :]
        fac = fac_ref[s]
        dproj = jnp.concatenate(
            [da * fac[0:128], da * fac[128:256], db * fac[256:384], db * fac[384:512]], axis=0
        ).astype(BF)
        dproj_ref[s] = dproj
        total += dot(dproj, norm_ref[s])
    sums[...] = total.astype(BF)
    last = pltpu.make_async_copy(sums, sum_hbm.at[pl.ds(0, 512)], sems.at[1])
    last.start()
    first.wait()
    last.wait()


def pair_kernel(dproj_ref, w_ref, dgate_ref, gw_ref, pair_ref, out_ref, token_ref):
    token_ref[...] = jnp.zeros((8, 128), F32)
    w = w_ref[...]
    gw = gw_ref[...]
    for s in range(8):
        zhat, zinv = layer_norm(pair_ref[:, s].astype(F32).reshape(128, 128))
        dnormed = dot(dproj_ref[s], w, ((0,), (1,))) + dot(dgate_ref[s], gw, ((0,), (1,)))
        grad = layer_norm_backward(dnormed, zhat, zinv)
        out_ref[:, s] = grad.reshape(4, 32, 128).astype(BF)


def sum_kernel(scale, parts_ref, out_ref):
    total = jnp.sum(parts_ref[...].astype(F32), axis=0, keepdims=True) * scale
    out_ref[...] = jnp.broadcast_to(total, out_ref.shape).astype(BF)


def collect_kernel(rows_ref, in_ref, gate_ref, out_ref):
    in_ref[...] = rows_ref[0:512].astype(F32).T
    gate_ref[...] = rows_ref[512:640].astype(F32)
    out_ref[...] = rows_ref[640:768].astype(F32)


def run(kernel, outs, *args, scratch=(), scalars=0, hbm=0, hbm_out=0, flops=0, after=(), grant=16):
    outs = [jax.ShapeDtypeStruct(shape, dtype) for shape, dtype in outs]
    vmem = pl.BlockSpec(memory_space=pltpu.VMEM)
    smem = pl.BlockSpec(memory_space=pltpu.SMEM)
    anywhere = pl.BlockSpec(memory_space=pltpu.HBM)
    skip = len(after)
    size = sum(v.size * v.dtype.itemsize for v in list(args) + outs)
    result = pl.pallas_call(
        lambda *refs: kernel(*refs[skip:]),
        out_shape=outs,
        in_specs=[anywhere] * (skip + hbm) + [smem] * scalars + [vmem] * (len(args) - scalars - hbm),
        out_specs=[anywhere] * hbm_out + [vmem] * (len(outs) - hbm_out),
        scratch_shapes=scratch,
        compiler_params=pltpu.CompilerParams(vmem_limit_bytes=grant * 1024 * 1024),
        cost_estimate=pl.CostEstimate(flops=flops, bytes_accessed=size, transcendentals=0),
    )(*after, *args)
    return result[0] if len(outs) == 1 else result


def exchange(values, axes):
    return lax.all_to_all(values, axes, 0, 0, tiled=True)


def per_device(pair, cotangent, in_weight, gate_weight, out_weight):
    core = jnp.reshape(lax.axis_index("core"), (1,)).astype(jnp.int32)
    pair = pair.reshape(4, 8, 32, 128)
    cotangent = cotangent.reshape(4, 8, 32, 128)

    msg, normed = run(
        project_kernel, [((128, 16, 128), BF), ((8, 128, 128), BF)], pair, in_weight, hbm=2, grant=56,
        scratch=[
            pltpu.VMEM((4, 8, 32, 128), BF), pltpu.VMEM((128, 512), BF),
            pltpu.VMEM((2048, 128), F32), pltpu.SemaphoreType.DMA((2,)),
        ],
        flops=134_000_000,
    )
    msg = exchange(msg, OWNERS).reshape(2, 8, 2, 4, 16, 128)
    g2, dout, dxnorm = run(
        side_kernel, [((8, 128, 128), F32), ((8, 128, 128), BF), ((1024, 128), F32)],
        normed, cotangent, gate_weight, out_weight, flops=67_000_000,
    )
    a_own, b_own, send = run(
        pack_kernel, [((512, 256), BF), ((2, 256, 256), BF), ((768, 256), BF)], core, msg, scalars=1,
        flops=1_000_000,
    )
    got = lax.ppermute(send, "core", SWAP)
    keep = run(keep_kernel, [((512, 256), F32)], core, a_own, b_own, scalars=1, flops=67_000_000)
    x = run(x_kernel, [((2, 16, 4, 8, 128), BF)], keep, got, flops=67_000_000)
    x = exchange(x.reshape(128, 8, 128), OWNERS)
    dx, xhat = run(
        dx_kernel, [((128, 8, 128), BF), ((128, 8, 128), F32)], x, dxnorm.reshape(128, 8, 128), flops=1_000_000
    )
    dx = exchange(dx, OWNERS)
    dx = dx.reshape(2, 16, 4, 8, 128)
    other = lax.ppermute(dx, "core", SWAP)
    sums, dgate, factors = run(
        late_kernel, [((256, 128), BF), ((8, 128, 128), BF), ((8, 512, 128), F32)],
        xhat.reshape(1024, 128), normed, g2, dout, in_weight, out_weight, flops=268_000_000,
    )
    dab = run(
        pull_kernel, [((2, 8, 2, 4, 16, 128), BF)], core, dx, other, a_own, b_own, scalars=1, after=(sums,),
        scratch=[pltpu.VMEM((2, 512, 256), BF), pltpu.VMEM((2, 8, 2, 4, 16, 128), F32)], flops=268_000_000,
    )
    dab = exchange(dab.reshape(128, 16, 128), OWNERS)
    parts, dproj = run(
        weight_kernel, [((768, 128), BF), ((8, 512, 128), BF)],
        sums, dab, factors, normed, hbm=1, hbm_out=1,
        scratch=[
            pltpu.VMEM((2048, 128), F32), pltpu.VMEM((512, 128), BF), pltpu.SemaphoreType.DMA((2,)),
        ],
        flops=134_000_000,
    )
    parts = exchange(parts.reshape(32, 24, 128), PLANE)
    pair_grad, token = run(
        pair_kernel, [((4, 8, 32, 128), BF), ((8, 128), F32)], dproj, in_weight, dgate, gate_weight, pair,
        flops=134_000_000,
    )
    parts = run(functools.partial(sum_kernel, 1.0), [((8, 24, 128), BF)], parts, after=(token,))
    parts = exchange(parts, LINE)
    parts = run(functools.partial(sum_kernel, 1.0 / 512), [((32, 24, 128), BF)], parts)
    whole = exchange(parts, PLANE).reshape(768, 128)
    in_grad, gate_grad, out_grad = run(
        collect_kernel, [((128, 512), F32), ((128, 128), F32), ((128, 128), F32)], whole
    )
    return (pair_grad.reshape(32, 32, 128), in_grad, gate_grad, out_grad)


def solution(mesh):
    fine = Mesh(mesh.devices.reshape(4, 4, 2, 4, 2), ALL)
    tiles = P(ROW, CHI + ("core",), None)
    return jax.shard_map(
        per_device,
        mesh=fine,
        in_specs=(tiles, tiles, P(), P(), P()),
        out_specs=(tiles, P(), P(), P()),
        check_vma=False,
    )
```

```python
import functools

import jax
import jax.numpy as jnp
from jax import lax
from jax.experimental import pallas as pl
from jax.experimental.pallas import tpu as pltpu
from jax.sharding import Mesh, PartitionSpec as P

ROW = ("y", "zh")
CHI = ("zl", "x")
OWNERS = ("zl", "y", "zh", "x")
PLANE = ("core", "y", "x")
LINE = ("zh", "zl")
ALL = ("y", "zh", "zl", "x", "core")
SWAP = [(0, 1), (1, 0)]
BF = jnp.bfloat16
F32 = jnp.float32
EPS = 1e-05


def dot(left, right, contract=((1,), (0,))):
    return lax.dot_general(left, right, (contract, ((), ())), preferred_element_type=F32)


def layer_norm(values, axis=-1):
    center = values - jnp.mean(values, axis=axis, keepdims=True)
    scale = lax.rsqrt(jnp.mean(center * center, axis=axis, keepdims=True) + EPS)
    return center * scale, scale


def layer_norm_backward(grad, normal, scale, axis=-1):
    first = jnp.mean(grad, axis=axis, keepdims=True)
    second = jnp.mean(grad * normal, axis=axis, keepdims=True)
    return scale * (grad - first - normal * second)


def regroup(parts):
    lane = lax.broadcasted_iota(jnp.int32, parts[0].shape, 1)
    low = lane < 64
    even = (lane // 32) % 2 == 0
    p0, p1, p2, p3 = parts
    roll = lambda v, n: pltpu.roll(v, n, 1)
    p0, p2 = jnp.where(low, p0, roll(p2, 64)), jnp.where(low, roll(p0, 64), p2)
    p1, p3 = jnp.where(low, p1, roll(p3, 64)), jnp.where(low, roll(p1, 64), p3)
    p0, p1 = jnp.where(even, p0, roll(p1, 32)), jnp.where(even, roll(p0, 96), p1)
    p2, p3 = jnp.where(even, p2, roll(p3, 32)), jnp.where(even, roll(p2, 96), p3)
    return [p0, p1, p2, p3]


def project_kernel(pair_hbm, w_hbm, msg_ref, norm_ref, pair_ref, w_ref, held, sems):
    copies = [
        pltpu.make_async_copy(pair_hbm, pair_ref, sems.at[0]),
        pltpu.make_async_copy(w_hbm, w_ref, sems.at[1]),
    ]
    for copy in copies:
        copy.start()
    for copy in copies:
        copy.wait()
    w = w_ref[...]
    pair = jnp.concatenate([pair_ref[:, s].astype(F32).reshape(128, 128) for s in range(8)], axis=0)
    normed = layer_norm(pair)[0].astype(BF)
    norm_ref[...] = normed.reshape(8, 128, 128)
    for n in range(2):
        val = dot(w[:, 256 * n : 256 * n + 128], normed, ((0,), (1,)))
        sig = jax.nn.sigmoid(dot(w[:, 256 * n + 128 : 256 * n + 256], normed, ((0,), (1,))))
        val = val * sig
        for s in range(8):
            held[pl.ds(8 * n + s, 128, stride=16), :] = val[:, 128 * s : 128 * s + 128]
    msg_ref[...] = held[...].reshape(128, 16, 128).astype(BF)


def side_kernel(norm_ref, cot_ref, gw_ref, ow_ref, g2_ref, dout_ref, dxn_ref):
    gw = gw_ref[...]
    ow = ow_ref[...]
    for s in range(8):
        gate = jax.nn.sigmoid(dot(norm_ref[s], gw))
        upstream = cot_ref[:, s].astype(F32).reshape(128, 128)
        dout = upstream * gate
        g2_ref[s] = (dout * (1.0 - gate)).T
        dout = dout.astype(BF)
        dout_ref[s] = dout
        dxn_ref[pl.ds(s, 128, stride=8), :] = dot(ow, dout, ((1,), (1,)))


def pack_a(msg_ref, a_ref):
    for t in range(2):
        parts = [msg_ref[t, :, :, q].astype(F32)[:, :, 0:8].reshape(128, 128) for q in range(4)]
        for g, part in enumerate(regroup(parts)):
            a_ref[pl.ds(128 * g, 128), pl.ds(128 * t, 128)] = part.astype(BF)


def pack_b(msg_ref, half, b_ref):
    for t in range(2):
        parts = [msg_ref[t, :, half, q].astype(F32)[:, 8:16].reshape(64, 128) for q in range(4)]
        parts = [part.reshape(8, 8, 128) for part in regroup(parts)]
        b_ref[:, pl.ds(128 * t, 128)] = jnp.stack(parts, axis=1).reshape(256, 128).astype(BF)


def pack_kernel(core_ref, msg_ref, a_ref, b_ref, send_ref):
    pack_a(msg_ref, a_ref)
    for half in range(2):
        pack_b(msg_ref, half, b_ref.at[half])
    send_ref[0:512] = a_ref[...]
    send_ref[512:768] = b_ref[1 - core_ref[0]]


def keep_kernel(core_ref, a_ref, b_ref, keep_ref):
    keep_ref[...] = dot(a_ref[...], b_ref[core_ref[0]], ((1,), (1,)))


def x_kernel(keep_ref, got_ref, msg_ref):
    x = keep_ref[...] + dot(got_ref[0:512], got_ref[512:768], ((1,), (1,)))
    for t in range(2):
        parts = [x[128 * g : 128 * g + 128, 128 * t : 128 * t + 128] for g in range(4)]
        for q, part in enumerate(regroup(parts)):
            msg_ref[t, :, q] = part.reshape(16, 8, 128).astype(BF)


def dx_kernel(x_ref, dxn_ref, msg_ref, xhat_ref):
    xhat, xinv = layer_norm(x_ref[...].astype(F32), 0)
    xhat_ref[...] = xhat
    msg_ref[...] = layer_norm_backward(dxn_ref[...], xhat, xinv, 0).astype(BF)


def pack_dx(ref, dx):
    for t in range(2):
        parts = [ref[t, :, q].astype(F32).reshape(128, 128) for q in range(4)]
        for g, part in enumerate(regroup(parts)):
            dx[pl.ds(128 * g, 128), pl.ds(128 * t, 128)] = part.astype(BF)


def late_kernel(
    own_ref, xhat_ref, norm_ref, g2_ref, dout_ref, w_ref, ow_ref, sum_ref, dgate_ref, fac_ref, dx_ref
):
    pack_dx(own_ref, dx_ref)
    w = w_ref[...]
    ow = ow_ref[...].T
    gate_part = jnp.zeros((128, 128), F32)
    out_part = jnp.zeros((128, 128), F32)
    for s in range(0, 8, 2):
        pair = (s, s + 1)
        normed = norm_ref[s : s + 2].reshape(256, 128)
        xnorm = jnp.concatenate([xhat_ref[pl.ds(n, 128, stride=8), :] for n in pair], axis=1).astype(BF)
        dgate = jnp.concatenate([g2_ref[n] for n in pair], axis=1) * dot(ow, xnorm)
        dgate = dgate.astype(BF)
        gate_part += dot(dgate, normed)
        out_part += dot(xnorm, dout_ref[s : s + 2].reshape(256, 128))
        proj = dot(w, normed, ((0,), (1,)))
        for m, n in enumerate(pair):
            lanes = slice(128 * m, 128 * m + 128)
            dgate_ref[n] = dgate[:, lanes]
            for k in range(2):
                val = proj[256 * k : 256 * k + 128, lanes]
                sig = jax.nn.sigmoid(proj[256 * k + 128 : 256 * k + 256, lanes])
                fac_ref[n, 256 * k : 256 * k + 128] = sig
                fac_ref[n, 256 * k + 128 : 256 * k + 256] = val * sig * (1.0 - sig)
    sum_ref[0:128] = gate_part.T.astype(BF)
    sum_ref[128:256] = out_part.astype(BF)


def pull_kernel(core_ref, own_ref, other_ref, a_ref, b_ref, msg_ref, dx, held):
    core = core_ref[0]
    pack_dx(other_ref, dx)
    da = dot(own_ref[...], b_ref[core]) + dot(dx[...], b_ref[1 - core])
    for t in range(2):
        parts = [da[128 * g : 128 * g + 128, 128 * t : 128 * t + 128] for g in range(4)]
        for q, part in enumerate(regroup(parts)):
            held[t, :, :, q, 0:8] = part.reshape(8, 2, 8, 128)
    for half in range(2):
        place = core if half == 0 else 1 - core
        part = own_ref[...] if half == 0 else dx[...]
        db = dot(part, a_ref[...], ((0,), (0,))).reshape(8, 4, 8, 256)
        for t in range(2):
            parts = [db[:, g, :, 128 * t : 128 * t + 128].reshape(64, 128) for g in range(4)]
            for q, part in enumerate(regroup(parts)):
                held[t, :, place, q, 8:16] = part.reshape(8, 8, 128)
    msg_ref[...] = held[...].astype(BF)


def weight_kernel(go_hbm, dab_ref, fac_ref, norm_ref, sum_hbm, dproj_ref, held, sums, sems):
    first = pltpu.make_async_copy(go_hbm, sum_hbm.at[pl.ds(512, 256)], sems.at[0])
    first.start()
    held[...] = dab_ref[...].astype(F32).reshape(2048, 128)
    total = jnp.zeros((512, 128), F32)
    for s in range(8):
        da = held[pl.ds(s, 128, stride=16), :]
        db = held[pl.ds(8 + s, 128, stride=16), :]
        fac = fac_ref[s]
        dproj = jnp.concatenate(
            [da * fac[0:128], da * fac[128:256], db * fac[256:384], db * fac[384:512]], axis=0
        ).astype(BF)
        dproj_ref[s] = dproj
        total += dot(dproj, norm_ref[s])
    sums[...] = total.astype(BF)
    last = pltpu.make_async_copy(sums, sum_hbm.at[pl.ds(0, 512)], sems.at[1])
    last.start()
    first.wait()
    last.wait()


def pair_kernel(dproj_ref, w_ref, dgate_ref, gw_ref, pair_ref, out_ref, token_ref):
    token_ref[...] = jnp.zeros((8, 128), F32)
    w = w_ref[...]
    gw = gw_ref[...]
    for s in range(8):
        zhat, zinv = layer_norm(pair_ref[:, s].astype(F32).reshape(128, 128))
        dnormed = dot(dproj_ref[s], w, ((0,), (1,))) + dot(dgate_ref[s], gw, ((0,), (1,)))
        grad = layer_norm_backward(dnormed, zhat, zinv)
        out_ref[:, s] = grad.reshape(4, 32, 128).astype(BF)


def sum_kernel(scale, parts_ref, out_ref):
    total = jnp.sum(parts_ref[...].astype(F32), axis=0, keepdims=True) * scale
    out_ref[...] = jnp.broadcast_to(total, out_ref.shape).astype(BF)


def collect_kernel(rows_ref, in_ref, gate_ref, out_ref):
    in_ref[...] = rows_ref[0:512].astype(F32).T
    gate_ref[...] = rows_ref[512:640].astype(F32)
    out_ref[...] = rows_ref[640:768].astype(F32)


def run(kernel, outs, *args, scratch=(), scalars=0, hbm=0, hbm_out=0, flops=0, after=(), grant=16):
    outs = [jax.ShapeDtypeStruct(shape, dtype) for shape, dtype in outs]
    vmem = pl.BlockSpec(memory_space=pltpu.VMEM)
    smem = pl.BlockSpec(memory_space=pltpu.SMEM)
    anywhere = pl.BlockSpec(memory_space=pltpu.HBM)
    skip = len(after)
    size = sum(v.size * v.dtype.itemsize for v in list(args) + outs)
    result = pl.pallas_call(
        lambda *refs: kernel(*refs[skip:]),
        out_shape=outs,
        in_specs=[anywhere] * (skip + hbm) + [smem] * scalars + [vmem] * (len(args) - scalars - hbm),
        out_specs=[anywhere] * hbm_out + [vmem] * (len(outs) - hbm_out),
        scratch_shapes=scratch,
        compiler_params=pltpu.CompilerParams(vmem_limit_bytes=grant * 1024 * 1024),
        cost_estimate=pl.CostEstimate(flops=flops, bytes_accessed=size, transcendentals=0),
    )(*after, *args)
    return result[0] if len(outs) == 1 else result


def exchange(values, axes):
    return lax.all_to_all(values, axes, 0, 0, tiled=True)


def per_device(pair, cotangent, in_weight, gate_weight, out_weight):
    core = jnp.reshape(lax.axis_index("core"), (1,)).astype(jnp.int32)
    pair = pair.reshape(4, 8, 32, 128)
    cotangent = cotangent.reshape(4, 8, 32, 128)

    msg, normed = run(
        project_kernel, [((128, 16, 128), BF), ((8, 128, 128), BF)], pair, in_weight, hbm=2, grant=56,
        scratch=[
            pltpu.VMEM((4, 8, 32, 128), BF), pltpu.VMEM((128, 512), BF),
            pltpu.VMEM((2048, 128), F32), pltpu.SemaphoreType.DMA((2,)),
        ],
        flops=134_000_000,
    )
    msg = exchange(msg, OWNERS).reshape(2, 8, 2, 4, 16, 128)
    g2, dout, dxnorm = run(
        side_kernel, [((8, 128, 128), F32), ((8, 128, 128), BF), ((1024, 128), F32)],
        normed, cotangent, gate_weight, out_weight, flops=67_000_000,
    )
    a_own, b_own, send = run(
        pack_kernel, [((512, 256), BF), ((2, 256, 256), BF), ((768, 256), BF)], core, msg, scalars=1,
        flops=1_000_000,
    )
    got = lax.ppermute(send, "core", SWAP)
    keep = run(keep_kernel, [((512, 256), F32)], core, a_own, b_own, scalars=1, flops=67_000_000)
    x = run(x_kernel, [((2, 16, 4, 8, 128), BF)], keep, got, flops=67_000_000)
    x = exchange(x.reshape(128, 8, 128), OWNERS)
    dx, xhat = run(
        dx_kernel, [((128, 8, 128), BF), ((128, 8, 128), F32)], x, dxnorm.reshape(128, 8, 128), flops=1_000_000
    )
    dx = exchange(dx, OWNERS)
    dx = dx.reshape(2, 16, 4, 8, 128)
    other = lax.ppermute(dx, "core", SWAP)
    sums, dgate, factors, own = run(
        late_kernel,
        [((256, 128), BF), ((8, 128, 128), BF), ((8, 512, 128), F32), ((512, 256), BF)],
        dx, xhat.reshape(1024, 128), normed, g2, dout, in_weight, out_weight, flops=268_000_000,
    )
    dab = run(
        pull_kernel, [((2, 8, 2, 4, 16, 128), BF)], core, own, other, a_own, b_own, scalars=1,
        scratch=[pltpu.VMEM((512, 256), BF), pltpu.VMEM((2, 8, 2, 4, 16, 128), F32)], flops=268_000_000,
    )
    dab = exchange(dab.reshape(128, 16, 128), OWNERS)
    parts, dproj = run(
        weight_kernel, [((768, 128), BF), ((8, 512, 128), BF)],
        sums, dab, factors, normed, hbm=1, hbm_out=1,
        scratch=[
            pltpu.VMEM((2048, 128), F32), pltpu.VMEM((512, 128), BF), pltpu.SemaphoreType.DMA((2,)),
        ],
        flops=134_000_000,
    )
    parts = exchange(parts.reshape(32, 24, 128), PLANE)
    pair_grad, token = run(
        pair_kernel, [((4, 8, 32, 128), BF), ((8, 128), F32)], dproj, in_weight, dgate, gate_weight, pair,
        flops=134_000_000,
    )
    parts = run(functools.partial(sum_kernel, 1.0), [((8, 24, 128), BF)], parts, after=(token,))
    parts = exchange(parts, LINE)
    parts = run(functools.partial(sum_kernel, 1.0 / 512), [((32, 24, 128), BF)], parts)
    whole = exchange(parts, PLANE).reshape(768, 128)
    in_grad, gate_grad, out_grad = run(
        collect_kernel, [((128, 512), F32), ((128, 128), F32), ((128, 128), F32)], whole
    )
    return (pair_grad.reshape(32, 32, 128), in_grad, gate_grad, out_grad)


def solution(mesh):
    fine = Mesh(mesh.devices.reshape(4, 4, 2, 4, 2), ALL)
    tiles = P(ROW, CHI + ("core",), None)
    return jax.shard_map(
        per_device,
        mesh=fine,
        in_specs=(tiles, tiles, P(), P(), P()),
        out_specs=(tiles, P(), P(), P()),
        check_vma=False,
    )
```

```python
import functools

import jax
import jax.numpy as jnp
from jax import lax
from jax.experimental import pallas as pl
from jax.experimental.pallas import tpu as pltpu
from jax.sharding import Mesh, PartitionSpec as P

ROW = ("y", "zh")
CHI = ("zl", "x")
OWNERS = ("zl", "y", "zh", "x")
PLANE = ("core", "y", "x")
LINE = ("zh", "zl")
ALL = ("y", "zh", "zl", "x", "core")
SWAP = [(0, 1), (1, 0)]
BF = jnp.bfloat16
F32 = jnp.float32
EPS = 1e-05


def dot(left, right, contract=((1,), (0,))):
    return lax.dot_general(left, right, (contract, ((), ())), preferred_element_type=F32)


def layer_norm(values, axis=-1):
    center = values - jnp.mean(values, axis=axis, keepdims=True)
    scale = lax.rsqrt(jnp.mean(center * center, axis=axis, keepdims=True) + EPS)
    return center * scale, scale


def layer_norm_backward(grad, normal, scale, axis=-1):
    first = jnp.mean(grad, axis=axis, keepdims=True)
    second = jnp.mean(grad * normal, axis=axis, keepdims=True)
    return scale * (grad - first - normal * second)


def regroup(parts):
    lane = lax.broadcasted_iota(jnp.int32, parts[0].shape, 1)
    low = lane < 64
    even = (lane // 32) % 2 == 0
    p0, p1, p2, p3 = parts
    roll = lambda v, n: pltpu.roll(v, n, 1)
    p0, p2 = jnp.where(low, p0, roll(p2, 64)), jnp.where(low, roll(p0, 64), p2)
    p1, p3 = jnp.where(low, p1, roll(p3, 64)), jnp.where(low, roll(p1, 64), p3)
    p0, p1 = jnp.where(even, p0, roll(p1, 32)), jnp.where(even, roll(p0, 96), p1)
    p2, p3 = jnp.where(even, p2, roll(p3, 32)), jnp.where(even, roll(p2, 96), p3)
    return [p0, p1, p2, p3]


def project_kernel(pair_hbm, w_hbm, msg_ref, norm_ref, pair_ref, w_ref, held, sems):
    copies = [
        pltpu.make_async_copy(pair_hbm, pair_ref, sems.at[0]),
        pltpu.make_async_copy(w_hbm, w_ref, sems.at[1]),
    ]
    for copy in copies:
        copy.start()
    for copy in copies:
        copy.wait()
    w = w_ref[...]
    pair = jnp.concatenate([pair_ref[:, s].astype(F32).reshape(128, 128) for s in range(8)], axis=0)
    ones = jnp.full((128, 128), 1.0, BF)
    center = pair - dot(pair.astype(BF), ones) * (1.0 / 128)
    scale = lax.rsqrt(jnp.mean(center * center, axis=-1, keepdims=True) + EPS)
    normed = (center * scale).astype(BF)
    norm_ref[...] = normed.reshape(8, 128, 128)
    for n in range(2):
        val = dot(w[:, 256 * n : 256 * n + 128], normed, ((0,), (1,)))
        sig = jax.nn.sigmoid(dot(w[:, 256 * n + 128 : 256 * n + 256], normed, ((0,), (1,))))
        val = val * sig
        for s in range(8):
            held[pl.ds(8 * n + s, 128, stride=16), :] = val[:, 128 * s : 128 * s + 128]
    msg_ref[...] = held[...].reshape(128, 16, 128).astype(BF)


def side_kernel(norm_ref, cot_ref, gw_ref, ow_ref, g2_ref, dout_ref, dxn_ref):
    gw = gw_ref[...]
    ow = ow_ref[...]
    for s in range(8):
        gate = jax.nn.sigmoid(dot(norm_ref[s], gw))
        upstream = cot_ref[:, s].astype(F32).reshape(128, 128)
        dout = upstream * gate
        g2_ref[s] = (dout * (1.0 - gate)).T
        dout = dout.astype(BF)
        dout_ref[s] = dout
        dxn_ref[pl.ds(s, 128, stride=8), :] = dot(ow, dout, ((1,), (1,)))


def pack_a(msg_ref, a_ref):
    for t in range(2):
        parts = [msg_ref[t, :, :, q].astype(F32)[:, :, 0:8].reshape(128, 128) for q in range(4)]
        for g, part in enumerate(regroup(parts)):
            a_ref[pl.ds(128 * g, 128), pl.ds(128 * t, 128)] = part.astype(BF)


def pack_b(msg_ref, half, b_ref):
    for t in range(2):
        parts = [msg_ref[t, :, half, q].astype(F32)[:, 8:16].reshape(64, 128) for q in range(4)]
        parts = [part.reshape(8, 8, 128) for part in regroup(parts)]
        b_ref[:, pl.ds(128 * t, 128)] = jnp.stack(parts, axis=1).reshape(256, 128).astype(BF)


def pack_kernel(core_ref, msg_ref, a_ref, b_ref, send_ref):
    pack_a(msg_ref, a_ref)
    for half in range(2):
        pack_b(msg_ref, half, b_ref.at[half])
    send_ref[0:512] = a_ref[...]
    send_ref[512:768] = b_ref[1 - core_ref[0]]


def keep_kernel(core_ref, a_ref, b_ref, keep_ref):
    keep_ref[...] = dot(a_ref[...], b_ref[core_ref[0]], ((1,), (1,)))


def x_kernel(keep_ref, got_ref, msg_ref):
    x = keep_ref[...] + dot(got_ref[0:512], got_ref[512:768], ((1,), (1,)))
    for t in range(2):
        parts = [x[128 * g : 128 * g + 128, 128 * t : 128 * t + 128] for g in range(4)]
        for q, part in enumerate(regroup(parts)):
            msg_ref[t, :, q] = part.reshape(16, 8, 128).astype(BF)


def dx_kernel(x_ref, dxn_ref, msg_ref, xhat_ref):
    xhat, xinv = layer_norm(x_ref[...].astype(F32), 0)
    xhat_ref[...] = xhat
    msg_ref[...] = layer_norm_backward(dxn_ref[...], xhat, xinv, 0).astype(BF)


def pack_dx(ref, dx):
    for t in range(2):
        parts = [ref[t, :, q].astype(F32).reshape(128, 128) for q in range(4)]
        for g, part in enumerate(regroup(parts)):
            dx[pl.ds(128 * g, 128), pl.ds(128 * t, 128)] = part.astype(BF)


def late_kernel(
    own_ref, xhat_ref, norm_ref, g2_ref, dout_ref, w_ref, ow_ref, sum_ref, dgate_ref, fac_ref, dx_ref
):
    pack_dx(own_ref, dx_ref)
    w = w_ref[...]
    ow = ow_ref[...].T
    gate_part = jnp.zeros((128, 128), F32)
    out_part = jnp.zeros((128, 128), F32)
    for s in range(0, 8, 2):
        pair = (s, s + 1)
        normed = norm_ref[s : s + 2].reshape(256, 128)
        xnorm = jnp.concatenate([xhat_ref[pl.ds(n, 128, stride=8), :] for n in pair], axis=1).astype(BF)
        dgate = jnp.concatenate([g2_ref[n] for n in pair], axis=1) * dot(ow, xnorm)
        dgate = dgate.astype(BF)
        gate_part += dot(dgate, normed)
        out_part += dot(xnorm, dout_ref[s : s + 2].reshape(256, 128))
        proj = dot(w, normed, ((0,), (1,)))
        for m, n in enumerate(pair):
            lanes = slice(128 * m, 128 * m + 128)
            dgate_ref[n] = dgate[:, lanes]
            for k in range(2):
                val = proj[256 * k : 256 * k + 128, lanes]
                sig = jax.nn.sigmoid(proj[256 * k + 128 : 256 * k + 256, lanes])
                fac_ref[n, 256 * k : 256 * k + 128] = sig
                fac_ref[n, 256 * k + 128 : 256 * k + 256] = val * sig * (1.0 - sig)
    sum_ref[0:128] = gate_part.T.astype(BF)
    sum_ref[128:256] = out_part.astype(BF)


def pull_kernel(core_ref, own_ref, other_ref, a_ref, b_ref, msg_ref, dx, held):
    core = core_ref[0]
    pack_dx(other_ref, dx)
    da = dot(own_ref[...], b_ref[core]) + dot(dx[...], b_ref[1 - core])
    for t in range(2):
        parts = [da[128 * g : 128 * g + 128, 128 * t : 128 * t + 128] for g in range(4)]
        for q, part in enumerate(regroup(parts)):
            held[t, :, :, q, 0:8] = part.reshape(8, 2, 8, 128)
    for half in range(2):
        place = core if half == 0 else 1 - core
        part = own_ref[...] if half == 0 else dx[...]
        db = dot(part, a_ref[...], ((0,), (0,))).reshape(8, 4, 8, 256)
        for t in range(2):
            parts = [db[:, g, :, 128 * t : 128 * t + 128].reshape(64, 128) for g in range(4)]
            for q, part in enumerate(regroup(parts)):
                held[t, :, place, q, 8:16] = part.reshape(8, 8, 128)
    msg_ref[...] = held[...].astype(BF)


def weight_kernel(go_hbm, dab_ref, fac_ref, norm_ref, sum_hbm, dproj_ref, held, sums, sems):
    first = pltpu.make_async_copy(go_hbm, sum_hbm.at[pl.ds(512, 256)], sems.at[0])
    first.start()
    held[...] = dab_ref[...].astype(F32).reshape(2048, 128)
    total = jnp.zeros((512, 128), F32)
    for s in range(8):
        da = held[pl.ds(s, 128, stride=16), :]
        db = held[pl.ds(8 + s, 128, stride=16), :]
        fac = fac_ref[s]
        dproj = jnp.concatenate(
            [da * fac[0:128], da * fac[128:256], db * fac[256:384], db * fac[384:512]], axis=0
        ).astype(BF)
        dproj_ref[s] = dproj
        total += dot(dproj, norm_ref[s])
    sums[...] = total.astype(BF)
    last = pltpu.make_async_copy(sums, sum_hbm.at[pl.ds(0, 512)], sems.at[1])
    last.start()
    first.wait()
    last.wait()


def pair_kernel(dproj_ref, w_ref, dgate_ref, gw_ref, pair_ref, out_ref, token_ref):
    token_ref[...] = jnp.zeros((8, 128), F32)
    w = w_ref[...]
    gw = gw_ref[...]
    for s in range(8):
        zhat, zinv = layer_norm(pair_ref[:, s].astype(F32).reshape(128, 128))
        dnormed = dot(dproj_ref[s], w, ((0,), (1,))) + dot(dgate_ref[s], gw, ((0,), (1,)))
        grad = layer_norm_backward(dnormed, zhat, zinv)
        out_ref[:, s] = grad.reshape(4, 32, 128).astype(BF)


def sum_kernel(scale, parts_ref, out_ref):
    total = jnp.sum(parts_ref[...].astype(F32), axis=0, keepdims=True) * scale
    out_ref[...] = jnp.broadcast_to(total, out_ref.shape).astype(BF)


def collect_kernel(rows_ref, in_ref, gate_ref, out_ref):
    in_ref[...] = rows_ref[0:512].astype(F32).T
    gate_ref[...] = rows_ref[512:640].astype(F32)
    out_ref[...] = rows_ref[640:768].astype(F32)


def run(kernel, outs, *args, scratch=(), scalars=0, hbm=0, hbm_out=0, flops=0, after=(), grant=16):
    outs = [jax.ShapeDtypeStruct(shape, dtype) for shape, dtype in outs]
    vmem = pl.BlockSpec(memory_space=pltpu.VMEM)
    smem = pl.BlockSpec(memory_space=pltpu.SMEM)
    anywhere = pl.BlockSpec(memory_space=pltpu.HBM)
    skip = len(after)
    size = sum(v.size * v.dtype.itemsize for v in list(args) + outs)
    result = pl.pallas_call(
        lambda *refs: kernel(*refs[skip:]),
        out_shape=outs,
        in_specs=[anywhere] * (skip + hbm) + [smem] * scalars + [vmem] * (len(args) - scalars - hbm),
        out_specs=[anywhere] * hbm_out + [vmem] * (len(outs) - hbm_out),
        scratch_shapes=scratch,
        compiler_params=pltpu.CompilerParams(vmem_limit_bytes=grant * 1024 * 1024),
        cost_estimate=pl.CostEstimate(flops=flops, bytes_accessed=size, transcendentals=0),
    )(*after, *args)
    return result[0] if len(outs) == 1 else result


def exchange(values, axes):
    return lax.all_to_all(values, axes, 0, 0, tiled=True)


def per_device(pair, cotangent, in_weight, gate_weight, out_weight):
    core = jnp.reshape(lax.axis_index("core"), (1,)).astype(jnp.int32)
    pair = pair.reshape(4, 8, 32, 128)
    cotangent = cotangent.reshape(4, 8, 32, 128)

    msg, normed = run(
        project_kernel, [((128, 16, 128), BF), ((8, 128, 128), BF)], pair, in_weight, hbm=2, grant=56,
        scratch=[
            pltpu.VMEM((4, 8, 32, 128), BF), pltpu.VMEM((128, 512), BF),
            pltpu.VMEM((2048, 128), F32), pltpu.SemaphoreType.DMA((2,)),
        ],
        flops=134_000_000,
    )
    msg = exchange(msg, OWNERS).reshape(2, 8, 2, 4, 16, 128)
    g2, dout, dxnorm = run(
        side_kernel, [((8, 128, 128), F32), ((8, 128, 128), BF), ((1024, 128), F32)],
        normed, cotangent, gate_weight, out_weight, flops=67_000_000,
    )
    a_own, b_own, send = run(
        pack_kernel, [((512, 256), BF), ((2, 256, 256), BF), ((768, 256), BF)], core, msg, scalars=1,
        flops=1_000_000,
    )
    got = lax.ppermute(send, "core", SWAP)
    keep = run(keep_kernel, [((512, 256), F32)], core, a_own, b_own, scalars=1, flops=67_000_000)
    x = run(x_kernel, [((2, 16, 4, 8, 128), BF)], keep, got, flops=67_000_000)
    x = exchange(x.reshape(128, 8, 128), OWNERS)
    dx, xhat = run(
        dx_kernel, [((128, 8, 128), BF), ((128, 8, 128), F32)], x, dxnorm.reshape(128, 8, 128), flops=1_000_000
    )
    dx = exchange(dx, OWNERS)
    dx = dx.reshape(2, 16, 4, 8, 128)
    other = lax.ppermute(dx, "core", SWAP)
    sums, dgate, factors, own = run(
        late_kernel,
        [((256, 128), BF), ((8, 128, 128), BF), ((8, 512, 128), F32), ((512, 256), BF)],
        dx, xhat.reshape(1024, 128), normed, g2, dout, in_weight, out_weight, flops=268_000_000,
    )
    dab = run(
        pull_kernel, [((2, 8, 2, 4, 16, 128), BF)], core, own, other, a_own, b_own, scalars=1,
        scratch=[pltpu.VMEM((512, 256), BF), pltpu.VMEM((2, 8, 2, 4, 16, 128), F32)], flops=268_000_000,
    )
    dab = exchange(dab.reshape(128, 16, 128), OWNERS)
    parts, dproj = run(
        weight_kernel, [((768, 128), BF), ((8, 512, 128), BF)],
        sums, dab, factors, normed, hbm=1, hbm_out=1,
        scratch=[
            pltpu.VMEM((2048, 128), F32), pltpu.VMEM((512, 128), BF), pltpu.SemaphoreType.DMA((2,)),
        ],
        flops=134_000_000,
    )
    parts = exchange(parts.reshape(32, 24, 128), PLANE)
    pair_grad, token = run(
        pair_kernel, [((4, 8, 32, 128), BF), ((8, 128), F32)], dproj, in_weight, dgate, gate_weight, pair,
        flops=134_000_000,
    )
    parts = run(functools.partial(sum_kernel, 1.0), [((8, 24, 128), BF)], parts, after=(token,))
    parts = exchange(parts, LINE)
    parts = run(functools.partial(sum_kernel, 1.0 / 512), [((32, 24, 128), BF)], parts)
    whole = exchange(parts, PLANE).reshape(768, 128)
    in_grad, gate_grad, out_grad = run(
        collect_kernel, [((128, 512), F32), ((128, 128), F32), ((128, 128), F32)], whole
    )
    return (pair_grad.reshape(32, 32, 128), in_grad, gate_grad, out_grad)


def solution(mesh):
    fine = Mesh(mesh.devices.reshape(4, 4, 2, 4, 2), ALL)
    tiles = P(ROW, CHI + ("core",), None)
    return jax.shard_map(
        per_device,
        mesh=fine,
        in_specs=(tiles, tiles, P(), P(), P()),
        out_specs=(tiles, P(), P(), P()),
        check_vma=False,
    )
```
